32 devices in a mesh: sample: 16 (over z, y, core), spatial: 2 (over x).
Axes of the slice: x: 2, y: 2, z: 4, core: 2. Of those that a mesh axis runs over, the one named last changes fastest.
Arguments:
- volume: bfloat16 [16, 32, 16, 1024], P('sample', 'spatial'), may hold values from -6 to 6
- w_first: bfloat16 [1728, 128], replicated, may hold values from -0.15625 to 0.15625
- w_second: bfloat16 [3456, 256], replicated, may hold values from -0.109375 to 0.109375
- cotangent: bfloat16 [16, 8, 4, 1024], P('sample', 'spatial'), may hold values from -0.13183594 to 0.13183594
Outputs:
- grad_first: float32 [1728, 128], replicated
- grad_second: float32 [3456, 256], replicated
The draws below stay inside these ranges and needn't reach their ends.
All inputs are finite; a program needn't handle non-finite values.
Results may differ from the reference program's by a relative error of at most 0.0052.
Values may be sent and summed in bfloat16 or wider, within the bound.
No kernel may reach another device: no remote copies, remote signals or barrier semaphores. Data moves between devices by JAX's collectives and lax.ppermute only.
A program may use at most 64 MiB of HBM per device.

```python
import jax
import jax.numpy as jnp
from jax import lax

C0 = 64
C1 = 128
C2 = 256
SZ = 32
SXY = 16
UNIVERSES = 16


def shard_levels(rng, dims, shards, low, high):
    def one(dim, blocks):
        steps = jax.random.uniform(jax.random.fold_in(jax.random.fold_in(rng, 6), dim), (blocks,), jnp.float32, low / len(shards), high / len(shards))
        return jnp.repeat(jnp.exp(steps), dims[dim] // blocks).reshape((-1,) + (1,) * (len(dims) - dim - 1))

    level = one(*shards[0])
    for cut in shards[1:]:
        level = level * one(*cut)
    return level


def normal_values(own_key, extent, spread, bound, cuts=(), held_as=jnp.bfloat16):
    entries = spread * jax.random.normal(own_key, extent, jnp.float32)
    if cuts:
        entries = entries * shard_levels(own_key, extent, cuts, -0.22, 0.18)
    return jnp.clip(entries, -bound, bound).astype(held_as)


def setup_inputs(seed: int = 0) -> dict:
    splits = jax.random.split(jax.random.key(seed), 5)
    return {
        "volume": normal_values(splits[0], (UNIVERSES, SZ, SXY, SXY * C0), 1.0, 6.0, ((0, 16), (1, 2))),
        "w_first": normal_values(splits[1], (27 * C0, C1), (27 * C0) ** -0.5, 0.15625),
        "w_second": normal_values(splits[2], (27 * C1, C2), (27 * C1) ** -0.5, 0.109375),
        "cotangent": normal_values(splits[3], (UNIVERSES, SZ // 4, SXY // 4, (SXY // 4) * C2), ((UNIVERSES * (SZ // 4) * (SXY // 4) ** 2) ** -0.5), 0.13183594, ((0, 16), (1, 2))),
    }


tap_offsets = [(first, second, third) for first in range(3) for second in range(3) for third in range(3)]


def silu_slope(value):
    sigmoid_value = jax.nn.sigmoid(value)
    return sigmoid_value * (1.0 + value * (1.0 - sigmoid_value))


def pad_cells(cells_in):
    return jnp.pad(cells_in, ((0, 0), (1, 1), (1, 1), (1, 1), (0, 0)))


def tap_slices(padded):
    batch_size, len_z, len_y, len_x, channels = padded.shape
    halves = padded.reshape(batch_size, len_z // 2, 2, len_y // 2, 2, len_x // 2, 2, channels)
    out_z, out_y, out_x = len_z // 2 - 1, len_y // 2 - 1, len_x // 2 - 1
    result = []
    for offset_z, offset_y, offset_x in tap_offsets:
        result.append(halves[:, offset_z // 2:offset_z // 2 + out_z, offset_z % 2, offset_y // 2:offset_y // 2 + out_y, offset_y % 2, offset_x // 2:offset_x // 2 + out_x, offset_x % 2, :])
    return result


def conv_taps(padded, weights):
    channels = padded.shape[-1]
    stacked = weights.reshape(27, channels, weights.shape[1])
    summed = None
    for tap_index, sliced in enumerate(tap_slices(padded)):
        product = jnp.dot(sliced, stacked[tap_index], preferred_element_type=jnp.float32)
        summed = product if summed is None else summed + product
    return summed


def weight_grads(padded, delta_cells):
    flat_grad = delta_cells.reshape(-1, delta_cells.shape[-1])
    blocks = []
    for sliced in tap_slices(padded):
        flat_in = sliced.reshape(-1, sliced.shape[-1])
        blocks.append(jnp.dot(flat_in.T, flat_grad, preferred_element_type=jnp.float32))
    return jnp.concatenate(blocks, axis=0)


def input_grads(delta_cells, weights):
    batch_size, out_z, out_y, out_x, outputs = delta_cells.shape
    channels = weights.shape[0] // 27
    stacked = weights.reshape(27, channels, outputs)
    parity_sums = {}
    for tap_index, (offset_z, offset_y, offset_x) in enumerate(tap_offsets):
        product = jnp.dot(delta_cells, stacked[tap_index].T, preferred_element_type=jnp.float32)
        placed = jnp.pad(product, ((0, 0), (offset_z // 2, 1 - offset_z // 2), (offset_y // 2, 1 - offset_y // 2), (offset_x // 2, 1 - offset_x // 2), (0, 0)))
        parity = (offset_z % 2, offset_y % 2, offset_x % 2)
        parity_sums[parity] = placed if parity not in parity_sums else parity_sums[parity] + placed
    planes = []
    for parity_z in range(2):
        rows_list = []
        for parity_y in range(2):
            rows_list.append(jnp.stack([parity_sums[(parity_z, parity_y, 0)], parity_sums[(parity_z, parity_y, 1)]], axis=4))
        planes.append(jnp.stack(rows_list, axis=3))
    joined = jnp.stack(planes, axis=2)
    return joined.reshape(batch_size, 2 * out_z + 2, 2 * out_y + 2, 2 * out_x + 2, channels)


def reference(volume, w_first, w_second, cotangent):
    def one_universe(carry, inputs):
        sample_in, sample_grad = inputs
        cells_in = sample_in.reshape(1, SZ, SXY, SXY, C0)
        padded_in = pad_cells(cells_in)
        first_pre = conv_taps(padded_in, w_first)
        hidden = jax.nn.silu(first_pre).astype(jnp.bfloat16)
        padded_hidden = pad_cells(hidden)
        second_pre = conv_taps(padded_hidden, w_second)
        upstream = sample_grad.reshape(second_pre.shape).astype(jnp.float32)
        second_delta = (upstream * silu_slope(second_pre)).astype(jnp.bfloat16)
        grad_second = weight_grads(padded_hidden, second_delta)
        hidden_grad = input_grads(second_delta, w_second)[:, 1:-1, 1:-1, 1:-1, :].astype(jnp.bfloat16)
        hidden_grad = lax.optimization_barrier(hidden_grad)
        first_delta = (hidden_grad.astype(jnp.float32) * silu_slope(first_pre)).astype(jnp.bfloat16)
        grad_first = weight_grads(padded_in, first_delta)
        return (carry[0] + grad_first, carry[1] + grad_second), None

    start = (jnp.zeros((27 * C0, C1), jnp.float32), jnp.zeros((27 * C1, C2), jnp.float32))
    totals, unused = lax.scan(one_universe, start, (volume, cotangent))
    return (totals[0], totals[1])
```

```python
import functools

import jax
import jax.numpy as jnp
from jax import lax
from jax.experimental import pallas as pl
from jax.experimental.pallas import tpu as pltpu
from jax.sharding import PartitionSpec as P

BOTH = ("sample", "spatial")
LANES = 128
VMEM_BYTES = 48 * 1024 * 1024
f32, bf16 = jnp.float32, jnp.bfloat16


def full(shape):
    return pl.BlockSpec(memory_space=pltpu.VMEM)


def params():
    return pltpu.CompilerParams(vmem_limit_bytes=VMEM_BYTES)


def call(kernel, outs, *args, scratch=(), cost=None):
    shapes = [jax.ShapeDtypeStruct(s, d) for s, d in outs]
    return pl.pallas_call(
        kernel,
        out_shape=shapes,
        in_specs=[full(a.shape) for a in args],
        out_specs=[full(s.shape) for s in shapes],
        scratch_shapes=scratch,
        compiler_params=params(),
        cost_estimate=cost,
    )(*args)


def flat_index(spatial_count):
    return lax.axis_index("sample") * spatial_count + lax.axis_index("spatial")


def bit_of(value, bit):
    return lax.rem(lax.div(value, jnp.int32(1 << bit)), jnp.int32(2))


def sigmoid(value):
    return 1.0 / (1.0 + jnp.exp(-value))


def slope_of(value, sig):
    return sig * (1.0 + value * (1.0 - sig))


def dot(a, b, dims=((1,), (0,))):
    return lax.dot_general(a, b, (dims, ((), ())), preferred_element_type=f32)


def selection():
    row = lax.broadcasted_iota(jnp.int32, (144, 64), 0)
    col = lax.broadcasted_iota(jnp.int32, (144, 64), 1)
    pair, cell = lax.div(row, 16), lax.rem(row, 16)
    b, c = lax.div(pair, 3), lax.rem(pair, 3)
    k, j = lax.div(cell, 4), lax.rem(cell, 4)
    x, y = lax.div(col, 8), lax.rem(col, 8)
    hit = (x == 2 * k + c - 1) & (y == 2 * j + b - 1)
    return hit.astype(f32).astype(bf16)


def main_kernel(
    core_bit, spatial_count, halo, vol, w1, w2, cot, keep, send, vpad, x1, w1p, x2, g1
):
    planes = vol.shape[0] + 3
    hidden_planes = (planes - 1) // 2
    out_planes = (hidden_planes - 1) // 2
    core = bit_of(flat_index(spatial_count), core_bit)
    vpad[:, :, 0:8, :] = jnp.zeros((planes, 8, 8, LANES), f32)
    for e in range(planes):
        plane = halo[e] if e < 3 else vol[e - 3]
        for kt in range(8):
            vpad[e, kt, 8:24, :] = plane[:, kt * LANES : (kt + 1) * LANES].astype(f32)
    for ab in range(9):
        w1p[ab * 256 : ab * 256 + 64, :] = jnp.zeros((64, 128), bf16)
        w1p[ab * 256 + 64 : (ab + 1) * 256, :] = w1[ab * 192 : (ab + 1) * 192, :]
    for e in range(planes):
        for b in range(3):
            tiles = [jnp.zeros((8, LANES), f32)]
            for kt in range(8):
                tiles.append(vpad[e, kt, pl.ds(7 + b, 8, stride=2), :])
            for kk in range(4):
                left = jnp.concatenate([tiles[2 * kk], tiles[2 * kk + 1]], 0).astype(bf16)
                right = jnp.concatenate([tiles[2 * kk + 1], tiles[2 * kk + 2]], 0).astype(bf16)
                for a in range(e % 2, 3, 2):
                    h = (e - a) // 2
                    if 0 <= h < hidden_planes:
                        rows = slice(h * 64 + kk * 16, h * 64 + kk * 16 + 16)
                        col = (a * 3 + b) * 256
                        x1[rows, col : col + LANES] = left
                        x1[rows, col + LANES : col + 2 * LANES] = right
    first_pre = dot(x1[...], w1p[...])
    sig = sigmoid(first_pre)
    hidden = (first_pre * sig).astype(bf16)
    slope1 = slope_of(first_pre, sig)
    select = selection()
    for h in range(hidden_planes):
        picked = dot(select, hidden[h * 64 : (h + 1) * 64]).astype(bf16)
        for a in range(h % 2, 3, 2):
            o = (h - a) // 2
            if 0 <= o < out_planes:
                for pair in range(9):
                    tap = a * 9 + pair
                    x2[o * 16 : (o + 1) * 16, tap * LANES : (tap + 1) * LANES] = picked[
                        pair * 16 : (pair + 1) * 16
                    ]
    second_pre = dot(x2[...], w2[...])
    sig2 = sigmoid(second_pre)
    delta2 = cot[...].astype(f32) * slope_of(second_pre, sig2)
    d2 = delta2.astype(bf16)
    lo, hi = delta2[:, :LANES], delta2[:, LANES:]
    own_first = jnp.concatenate(
        [jnp.where(core == 0, lo, hi), jnp.where(core == 0, hi, lo)], 1
    ).astype(bf16)
    taps = 9 * LANES
    for a in range(3):
        grad = dot(x2[:, a * taps : (a + 1) * taps], own_first, ((0,), (0,)))
        keep[a, 0:taps, :] = grad[:, :LANES]
        send[a, 0:taps, :] = grad[:, LANES:].astype(bf16)
    spread = dot(d2, w2[...], ((1,), (1,)))
    coarse = spread.astype(bf16)
    fine = (spread - coarse.astype(f32)).astype(bf16)
    deltas = []
    for h in range(hidden_planes):
        total = None
        for a in range(h % 2, 3, 2):
            o = (h - a) // 2
            if 0 <= o < out_planes:
                for piece in (coarse, fine):
                    stack = jnp.concatenate(
                        [
                            piece[o * 16 : (o + 1) * 16, tap * LANES : (tap + 1) * LANES]
                            for tap in range(a * 9, a * 9 + 9)
                        ],
                        0,
                    )
                    part = dot(select, stack, ((0,), (0,)))
                    total = part if total is None else total + part
        rounded = total.astype(bf16).astype(f32)
        deltas.append((rounded * slope1[h * 64 : (h + 1) * 64]).astype(bf16))
    d1 = jnp.concatenate(deltas, 0)
    half = 288
    for a in range(3):
        grad = dot(x1[:, a * 768 : (a + 1) * 768], d1, ((0,), (0,)))
        for b in range(3):
            g1[b * 192 : (b + 1) * 192, :] = grad[b * 256 + 64 : (b + 1) * 256]
        keep[a, taps : taps + half, :] = g1[pl.ds(core * half, half), :]
        send[a, taps : taps + half, :] = g1[pl.ds((1 - core) * half, half), :].astype(bf16)
        rest = keep.shape[1] - taps - half
        keep[a, taps + half :, :] = jnp.zeros((rest, LANES), f32)
        send[a, taps + half :, :] = jnp.zeros((rest, LANES), bf16)


def reduce_kernel(orders, step, spatial_count, merged_in, merged_out, keep, *refs):
    lanes = len(orders)
    recv = refs[:1] if merged_in else refs[:lanes]
    outs = refs[len(recv) :]
    half = keep.shape[1] // 2
    flat = flat_index(spatial_count)
    for t in range(lanes):
        bit = bit_of(flat, orders[t][step])
        mine, other = pl.ds(bit * half, half), pl.ds((1 - bit) * half, half)
        if merged_in:
            got_mine, got_other = recv[0][t, mine, :], recv[0][t, other, :]
        else:
            got_mine, got_other = recv[t][mine, :], recv[t][other, :]
        outs[0][t] = keep[t, mine, :] + got_mine.astype(f32)
        gone = (keep[t, other, :] + got_other.astype(f32)).astype(bf16)
        if merged_out:
            outs[1][t] = gone
        else:
            outs[1 + t][...] = gone


def last_sum_kernel(merged_in, keep, *refs):
    out = refs[-1]
    for t in range(keep.shape[0]):
        got = refs[0][t] if merged_in else refs[t][...]
        out[t] = (keep[t] + got.astype(f32)).astype(bf16)


def final_kernel(core_bit, orders, chunk, spatial_count, *refs):
    lanes = len(orders)
    own, got, (grad_first, grad_second) = refs[:lanes], refs[lanes : 2 * lanes], refs[2 * lanes :]
    flat = flat_index(spatial_count)
    core = bit_of(flat, core_bit)
    taps, half = 9 * LANES, 288
    for t in range(lanes):
        steps = len(orders[t])
        bits = [bit_of(flat, orders[t][s]) for s in range(steps)]
        for place in range((taps + half) // chunk):
            position = jnp.int32(0)
            for s in range(steps):
                want = (place >> (steps - 1 - s)) & 1
                differs = (1 - bits[s]) if want else bits[s]
                position = position + differs * (1 << (steps - 1 - s))
            rows = pl.ds(position * chunk, chunk)
            a_half, b_half = own[t][rows, :].astype(f32), got[t][rows, :].astype(f32)
            low = jnp.where(core == 0, a_half, b_half)
            high = jnp.where(core == 0, b_half, a_half)
            at = place * chunk
            if at < taps:
                grad_second[t * taps + at : t * taps + at + chunk, :LANES] = low
                grad_second[t * taps + at : t * taps + at + chunk, LANES:] = high
            else:
                at = t * 2 * half + at - taps
                grad_first[at : at + chunk, :] = low
                grad_first[at + half : at + half + chunk, :] = high


def body(spatial_count, sample_count, volume, w_first, w_second, cotangent):
    count = spatial_count * sample_count
    bits = count.bit_length() - 1
    core_bit = spatial_count.bit_length() - 1
    others = [bit for bit in range(bits) if bit != core_bit]
    turn, rest = others[:3], others[3:]
    orders = [tuple(turn[t:] + turn[:t] + rest) for t in range(3)]
    steps = len(others)
    same = [len({order[s] for order in orders}) == 1 for s in range(steps)]
    chunk = -(-1440 // (16 << steps)) * 16
    rows = chunk << steps

    def swap(array, bit):
        return lax.ppermute(array, BOTH, [(i, i ^ (1 << bit)) for i in range(count)])

    slab = volume[0]
    planes = slab.shape[0] + 3
    hidden_planes = (planes - 1) // 2
    out_planes = (hidden_planes - 1) // 2
    halo = lax.ppermute(slab[-3:], "spatial", [(i, i + 1) for i in range(spatial_count - 1)])
    cot = cotangent[0].reshape(out_planes, 4, 4, 256).transpose(0, 2, 1, 3)
    cot = cot.reshape(out_planes * 16, 256)
    keep, send = call(
        functools.partial(main_kernel, core_bit, spatial_count),
        [((3, rows, LANES), f32), ((3, rows, LANES), bf16)],
        halo,
        slab,
        w_first,
        w_second,
        cot,
        scratch=[
            pltpu.VMEM((planes, 8, 24, LANES), f32),
            pltpu.VMEM((hidden_planes * 64, 9 * 256), bf16),
            pltpu.VMEM((9 * 256, 128), bf16),
            pltpu.VMEM((out_planes * 16, 27 * LANES), bf16),
            pltpu.VMEM((576, LANES), f32),
        ],
    )
    recv = [swap(send, core_bit)]
    merged = True
    for step in range(steps):
        half = keep.shape[1] // 2
        outs = [((3, half, LANES), f32)]
        outs += [((3, half, LANES), bf16)] if same[step] else [((half, LANES), bf16)] * 3
        keep, *send = call(
            functools.partial(reduce_kernel, orders, step, spatial_count, merged, same[step]),
            outs,
            keep,
            *recv,
        )
        merged = same[step]
        if merged:
            recv = [swap(send[0], orders[0][step])]
        else:
            recv = [swap(send[t], orders[t][step]) for t in range(3)]
    own = call(
        functools.partial(last_sum_kernel, merged), [((3, chunk, LANES), bf16)], keep, *recv
    )[0]
    for step in reversed(range(steps)):
        if same[step]:
            got = swap(own, orders[0][step])
            own = jnp.concatenate([own, got], 1)
        else:
            got = [swap(own[t], orders[t][step]) for t in range(3)]
            own = [jnp.concatenate([own[t], got[t]], 0) for t in range(3)]
    got = [swap(own[t], core_bit) for t in range(3)]
    return call(
        functools.partial(final_kernel, core_bit, orders, chunk, spatial_count),
        [((1728, 128), f32), ((3456, 256), f32)],
        *[own[t] for t in range(3)],
        *got,
    )


def solution(mesh):
    sizes = dict(mesh.shape)

    def run(*args):
        return tuple(body(sizes["spatial"], sizes["sample"], *args))

    return jax.shard_map(
        run,
        mesh=mesh,
        in_specs=(P("sample", "spatial", None, None), P(), P(), P("sample", "spatial", None, None)),
        out_specs=(P(), P()),
        check_vma=False,
    )
```

```python
import functools

import jax
import jax.numpy as jnp
from jax import lax
from jax.experimental import pallas as pl
from jax.experimental.pallas import tpu as pltpu
from jax.sharding import PartitionSpec as P

BOTH = ("sample", "spatial")
LANES = 128
SECOND, FIRST = 3456, 864
VMEM_BYTES = 32 * 1024 * 1024
SPLIT = 17
LANE_TURNS = (((0, 1, 2), (1, 2, 0)), ((2, 0, 1), (1, 0, 2)))
f32, bf16 = jnp.float32, jnp.bfloat16


def full(shape):
    return pl.BlockSpec(memory_space=pltpu.VMEM)


def params():
    return pltpu.CompilerParams(vmem_limit_bytes=VMEM_BYTES)


def call(kernel, outs, *args, specs=None, scratch=(), cost=None):
    shapes = [jax.ShapeDtypeStruct(s, d) for s, d in outs]
    return pl.pallas_call(
        kernel,
        out_shape=shapes,
        in_specs=specs or [full(a.shape) for a in args],
        out_specs=[full(s.shape) for s in shapes],
        scratch_shapes=scratch,
        compiler_params=params(),
        cost_estimate=cost,
    )(*args)


def flat_index(spatial_count):
    return lax.axis_index("sample") * spatial_count + lax.axis_index("spatial")


def bit_of(value, bit):
    return lax.rem(lax.div(value, jnp.int32(1 << bit)), jnp.int32(2))


def sigmoid(value):
    return 1.0 / (1.0 + jnp.exp(-value))


def slope_of(value, sig):
    return sig * (1.0 + value * (1.0 - sig))


def dot(a, b, dims=((1,), (0,))):
    return lax.dot_general(a, b, (dims, ((), ())), preferred_element_type=f32)


def selection():
    row = lax.broadcasted_iota(jnp.int32, (144, 64), 0)
    col = lax.broadcasted_iota(jnp.int32, (144, 64), 1)
    pair, cell = lax.div(row, 16), lax.rem(row, 16)
    b, c = lax.div(pair, 3), lax.rem(pair, 3)
    k, j = lax.div(cell, 4), lax.rem(cell, 4)
    x, y = lax.div(col, 8), lax.rem(col, 8)
    hit = (x == 2 * k + c - 1) & (y == 2 * j + b - 1)
    return hit.astype(f32).astype(bf16)


def fill(vpad, x1, planes, first_hidden, count):
    for index, (e, plane) in enumerate(planes):
        vpad[index, :, 0:8, :] = jnp.zeros((8, 8, LANES), f32)
        for kt in range(8):
            vpad[index, kt, 8:24, :] = plane[:, kt * LANES : (kt + 1) * LANES].astype(f32)
    for index, (e, plane) in enumerate(planes):
        for b in range(3):
            tiles = [jnp.zeros((8, LANES), f32)]
            for kt in range(8):
                tiles.append(vpad[index, kt, pl.ds(7 + b, 8, stride=2), :])
            for kk in range(4):
                left = jnp.concatenate([tiles[2 * kk], tiles[2 * kk + 1]], 0).astype(bf16)
                right = jnp.concatenate([tiles[2 * kk + 1], tiles[2 * kk + 2]], 0).astype(bf16)
                for a in range(e % 2, 3, 2):
                    h = (e - a) // 2 - first_hidden
                    if 0 <= h < count:
                        rows = slice(h * 64 + kk * 16, h * 64 + kk * 16 + 16)
                        col = (a * 3 + b) * 256
                        x1[rows, col : col + LANES] = left
                        x1[rows, col + LANES : col + 2 * LANES] = right


def load_kernel(vol_hbm, w1_hbm, face, low, x1, w1p, vol, w1, vpad, sems):
    loads = [
        pltpu.make_async_copy(vol_hbm, vol, sems.at[0]),
        pltpu.make_async_copy(w1_hbm, w1, sems.at[1]),
    ]
    for load in loads:
        load.start()
    loads[0].wait()
    depth = vol.shape[0]
    face[...] = vol[depth - 3 : depth]
    low[...] = vol[0:2]
    planes = [(e, vol[e - 3]) for e in range(4, depth + 3)]
    fill(vpad, x1, planes, 2, x1.shape[0] // 64)
    loads[1].wait()
    for ab in range(9):
        w1p[ab * 256 : ab * 256 + 64, :] = jnp.zeros((64, 128), bf16)
        w1p[ab * 256 + 64 : (ab + 1) * 256, :] = w1[ab * 192 : (ab + 1) * 192, :]


def hidden_of(x1, w1p, slope, picked):
    first_pre = dot(x1[...], w1p[...])
    sig = sigmoid(first_pre)
    hidden = (first_pre * sig).astype(bf16)
    slope[...] = slope_of(first_pre, sig)
    select = selection()
    for h in range(hidden.shape[0] // 64):
        picked[h * 144 : (h + 1) * 144, :] = dot(
            select, hidden[h * 64 : (h + 1) * 64]
        ).astype(bf16)


def upper_kernel(x1, w1p, w2_hbm, slope, picked, w2, sem):
    load = pltpu.make_async_copy(w2_hbm, w2, sem)
    load.start()
    hidden_of(x1, w1p, slope, picked)
    load.wait()


def second_taps(x2, own_first, keep, send, first_tap, last_tap):
    columns = slice(first_tap * LANES, last_tap * LANES)
    rows = (last_tap - first_tap) * LANES
    grad = dot(x2[:, columns], own_first, ((0,), (0,)))
    keep[0:rows, :] = grad[:, :LANES]
    send[0:rows, :] = grad[:, LANES:].astype(bf16)


def clear(keep, send, start):
    if start < keep.shape[0]:
        keep[start:, :] = jnp.zeros((keep.shape[0] - start, LANES), f32)
        send[start:, :] = jnp.zeros((keep.shape[0] - start, LANES), bf16)


def lower_kernel(
    core_bit, spatial_count, halo, low, w1p, picked_up, w2, cot,
    keep, send, x1, slope, x2, d2, own_first, vpad, picked,
):
    planes = [(e, halo[e]) for e in range(3)] + [(e, low[e - 3]) for e in (3, 4)]
    fill(vpad, x1, planes, 0, 2)
    hidden_of(x1, w1p, slope, picked)
    out_planes = x2.shape[0] // 16
    for o in range(out_planes):
        for tap in range(27):
            h, pair = 2 * o + tap // 9, tap % 9
            if h < 2:
                cells = picked[h * 144 + pair * 16 : h * 144 + (pair + 1) * 16, :]
            else:
                at = (h - 2) * 144 + pair * 16
                cells = picked_up[at : at + 16, :]
            x2[o * 16 : (o + 1) * 16, tap * LANES : (tap + 1) * LANES] = cells
    second_pre = dot(x2[...], w2[...])
    sig = sigmoid(second_pre)
    delta = cot[...].astype(f32) * slope_of(second_pre, sig)
    d2[...] = delta.astype(bf16)
    core = bit_of(flat_index(spatial_count), core_bit)
    left, right = delta[:, :LANES], delta[:, LANES:]
    own_first[...] = jnp.concatenate(
        [jnp.where(core == 0, left, right), jnp.where(core == 0, right, left)], 1
    ).astype(bf16)
    second_taps(x2, own_first[...], keep, send, 0, SPLIT)
    clear(keep, send, SPLIT * LANES)


def last_kernel(
    core_bit, spatial_count, x1_up, x1_low, slope_up, slope_low, x2, d2, own_first, w2,
    keep, send, g1,
):
    second_taps(x2, own_first[...], keep, send, SPLIT, 27)
    out_planes = x2.shape[0] // 16
    hidden_planes = 2 * out_planes + 1
    select = selection()
    spread = dot(d2[...], w2[...], ((1,), (1,)))
    coarse = spread.astype(bf16)
    fine = (spread - coarse.astype(f32)).astype(bf16)
    deltas = []
    for h in range(hidden_planes):
        total = None
        for a in range(h % 2, 3, 2):
            o = (h - a) // 2
            if 0 <= o < out_planes:
                for piece in (coarse, fine):
                    stack = jnp.concatenate(
                        [
                            piece[o * 16 : (o + 1) * 16, tap * LANES : (tap + 1) * LANES]
                            for tap in range(a * 9, a * 9 + 9)
                        ],
                        0,
                    )
                    part = dot(select, stack, ((0,), (0,)))
                    total = part if total is None else total + part
        rounded = total.astype(bf16).astype(f32)
        if h < 2:
            slope = slope_low[h * 64 : (h + 1) * 64]
        else:
            slope = slope_up[(h - 2) * 64 : (h - 1) * 64]
        deltas.append((rounded * slope).astype(bf16))
    d1_low, d1_up = jnp.concatenate(deltas[:2], 0), jnp.concatenate(deltas[2:], 0)
    for a in range(3):
        columns = slice(a * 768, (a + 1) * 768)
        grad = dot(x1_up[:, columns], d1_up, ((0,), (0,)))
        grad = grad + dot(x1_low[:, columns], d1_low, ((0,), (0,)))
        for b in range(3):
            at = (a * 3 + b) * 192
            g1[at : at + 192, :] = grad[b * 256 + 64 : (b + 1) * 256]
    core = bit_of(flat_index(spatial_count), core_bit)
    start = (27 - SPLIT) * LANES
    mine = pl.ds(pl.multiple_of(core * FIRST, 8), FIRST)
    other = pl.ds(pl.multiple_of((1 - core) * FIRST, 8), FIRST)
    keep[start : start + FIRST, :] = g1[mine, :]
    send[start : start + FIRST, :] = g1[other, :].astype(bf16)
    clear(keep, send, start + FIRST)


def side_of(flat, orders, core, step):
    first, second = bit_of(flat, orders[0][step]), bit_of(flat, orders[1][step])
    return jnp.where(core == 0, first, second)


def reduce_kernel(orders, core_bit, step, spatial_count, keep, recv, kept, gone):
    half = keep.shape[0] // 2
    flat = flat_index(spatial_count)
    bit = side_of(flat, orders, bit_of(flat, core_bit), step)
    mine = pl.ds(pl.multiple_of(bit * half, 16), half)
    other = pl.ds(pl.multiple_of((1 - bit) * half, 16), half)
    kept[...] = keep[mine, :] + recv[mine, :].astype(f32)
    gone[...] = (keep[other, :] + recv[other, :].astype(f32)).astype(bf16)


def sum_kernel(keep, recv, out):
    out[...] = (keep[...].astype(f32) + recv[...].astype(f32)).astype(bf16)


def final_kernel(core_bit, orders, chunk, spatial_count, own, segments, *refs):
    part, grad_first, grad_second, wide, sems = refs[0], *refs[-4:]
    flat = flat_index(spatial_count)
    core = bit_of(flat, core_bit)
    side = core if own else 1 - core
    steps = len(orders[0]) - 1
    bits = [side_of(flat, orders, side, s) for s in range(steps)]
    columns = pl.ds(pl.multiple_of(side * LANES, LANES), LANES)
    copies = []
    for place in range(1 << steps):
        position = jnp.int32(0)
        for s in range(steps):
            want = (place >> (steps - 1 - s)) & 1
            differs = (1 - bits[s]) if want else bits[s]
            position = position + differs * (1 << (steps - 1 - s))
        rows = pl.ds(pl.multiple_of(position * chunk, 16), chunk)
        at = place * chunk
        wide[at : at + chunk, :] = part[rows, :].astype(f32)
        for start, size, second, base in segments:
            low, high = max(start, at), min(start + size, at + chunk)
            if low >= high:
                continue
            to = base + low - start
            if second:
                target = grad_second.at[to : to + high - low, columns]
            else:
                target = grad_first.at[
                    pl.ds(pl.multiple_of(side * FIRST + to, 16), high - low)
                ]
            copy = pltpu.make_async_copy(wide.at[low:high], target, sems.at[len(copies)])
            copy.start()
            copies.append(copy)
    for copy in copies:
        copy.wait()


def body(spatial_count, sample_count, volume, w_first, w_second, cotangent):
    count = spatial_count * sample_count
    bits = count.bit_length() - 1
    core_bit = spatial_count.bit_length() - 1
    others = [bit for bit in range(bits) if bit != core_bit]
    turn, rest = others[:3], others[3:]
    orders = [
        [tuple(turn[i] for i in turns) + tuple(rest) for turns in lane] for lane in LANE_TURNS
    ]
    steps = len(others) - 1
    unit = 16 << steps
    second_rest = (27 - SPLIT) * LANES
    segments = [
        [(0, SPLIT * LANES, True, 0)],
        [(0, second_rest, True, SPLIT * LANES), (second_rest, FIRST, False, 0)],
    ]
    chunks = [-(-sum(seg[1] for seg in lane) // unit) * 16 for lane in segments]

    def swap_core(array):
        return lax.ppermute(array, BOTH, [(i, i ^ (1 << core_bit)) for i in range(count)])

    def swap(array, lane, step):
        pairs = [(i, i ^ (1 << orders[lane][(i >> core_bit) & 1][step])) for i in range(count)]
        return lax.ppermute(array, BOTH, pairs)

    slab = volume[0]
    depth = slab.shape[0]
    out_planes = depth // 4
    up = 2 * out_planes - 1
    cot = cotangent[0].reshape(out_planes, 4, 4, 256).transpose(0, 2, 1, 3)
    cot = cot.reshape(out_planes * 16, 256)
    outside = pl.BlockSpec(memory_space=pl.ANY)
    face, low, x1_up, w1p = call(
        load_kernel,
        [
            ((3, 16, 1024), bf16),
            ((2, 16, 1024), bf16),
            ((up * 64, 9 * 256), bf16),
            ((9 * 256, 128), bf16),
        ],
        slab,
        w_first,
        specs=[outside, outside],
        scratch=[
            pltpu.VMEM(slab.shape, bf16),
            pltpu.VMEM(w_first.shape, bf16),
            pltpu.VMEM((depth - 1, 8, 24, LANES), f32),
            pltpu.SemaphoreType.DMA((2,)),
        ],
    )
    halo = lax.ppermute(face, "spatial", [(i, i + 1) for i in range(spatial_count - 1)])
    slope_up, picked_up, w2 = call(
        upper_kernel,
        [((up * 64, LANES), f32), ((up * 144, LANES), bf16), (w_second.shape, bf16)],
        x1_up,
        w1p,
        w_second,
        specs=[full(None), full(None), outside],
        scratch=[pltpu.SemaphoreType.DMA],
        cost=pl.CostEstimate(flops=4 * 10**8, bytes_accessed=10**7, transcendentals=0),
    )
    rows = [chunk << steps for chunk in chunks]
    cells = out_planes * 16
    keep0, send0, x1_low, slope_low, x2, d2, own_first = call(
        functools.partial(lower_kernel, core_bit, spatial_count),
        [
            ((rows[0], LANES), f32),
            ((rows[0], LANES), bf16),
            ((128, 9 * 256), bf16),
            ((128, LANES), f32),
            ((cells, 27 * LANES), bf16),
            ((cells, 256), bf16),
            ((cells, 256), bf16),
        ],
        halo,
        low,
        w1p,
        picked_up,
        w2,
        cot,
        scratch=[pltpu.VMEM((5, 8, 24, LANES), f32), pltpu.VMEM((288, LANES), bf16)],
    )
    recv0 = swap_core(send0)
    keep1, send1 = call(
        functools.partial(last_kernel, core_bit, spatial_count),
        [((rows[1], LANES), f32), ((rows[1], LANES), bf16)],
        x1_up,
        x1_low,
        slope_up,
        slope_low,
        x2,
        d2,
        own_first,
        w2,
        scratch=[pltpu.VMEM((2 * FIRST, LANES), f32)],
        cost=pl.CostEstimate(flops=10**9, bytes_accessed=10**7, transcendentals=0),
    )
    recv1 = swap_core(send1)
    keep, recv, own = [keep0, keep1], [recv0, recv1], [None, None]
    for step in range(steps):
        for lane in range(2):
            half = keep[lane].shape[0] // 2
            keep[lane], send = call(
                functools.partial(reduce_kernel, orders[lane], core_bit, step, spatial_count),
                [((half, LANES), f32), ((half, LANES), bf16)],
                keep[lane],
                recv[lane],
            )
            recv[lane] = swap(send, lane, step)
    for lane in range(2):
        shape = [((chunks[lane], LANES), bf16)]
        own[lane] = call(sum_kernel, shape, keep[lane], recv[lane])[0]
        own[lane] = call(sum_kernel, shape, own[lane], swap(own[lane], lane, steps))[0]
    for step in reversed(range(steps)):
        for lane in range(2):
            own[lane] = jnp.concatenate([own[lane], swap(own[lane], lane, step)], 0)
    got = [swap_core(own[lane]) for lane in range(2)]
    shapes = [jax.ShapeDtypeStruct((2 * FIRST, LANES), f32)]
    shapes += [jax.ShapeDtypeStruct((SECOND, 2 * LANES), f32)]
    grads = ()
    for lane in range(2):
        for mine in (True, False):
            part = own[lane] if mine else got[lane]
            grads = pl.pallas_call(
                functools.partial(
                    final_kernel, core_bit, orders[lane], chunks[lane], spatial_count, mine,
                    segments[lane],
                ),
                out_shape=shapes,
                in_specs=[full(part.shape)] + [outside] * len(grads),
                out_specs=[outside] * 2,
                scratch_shapes=[
                    pltpu.VMEM((rows[lane], LANES), f32),
                    pltpu.SemaphoreType.DMA(((1 << steps) + 1,)),
                ],
                input_output_aliases={1: 0, 2: 1} if grads else {},
                compiler_params=params(),
            )(part, *grads)
    return grads


def solution(mesh):
    sizes = dict(mesh.shape)

    def run(*args):
        return tuple(body(sizes["spatial"], sizes["sample"], *args))

    return jax.shard_map(
        run,
        mesh=mesh,
        in_specs=(P("sample", "spatial", None, None), P(), P(), P("sample", "spatial", None, None)),
        out_specs=(P(), P()),
        check_vma=False,
    )
```

```python
import functools

import jax
import jax.numpy as jnp
from jax import lax
from jax.experimental import pallas as pl
from jax.experimental.pallas import tpu as pltpu
from jax.sharding import PartitionSpec as P

BOTH = ("sample", "spatial")
LANES = 128
SECOND, FIRST = 3456, 864
VMEM_BYTES = 32 * 1024 * 1024
SPLIT = 17
LANE_TURNS = (((0, 1, 2), (2, 0, 1)), ((1, 2, 0), (2, 0, 1)))
f32, bf16 = jnp.float32, jnp.bfloat16

STEP_COST = pl.CostEstimate(flops=4 * 10**9, bytes_accessed=8 * 10**7, transcendentals=0)


def full(shape):
    return pl.BlockSpec(memory_space=pltpu.VMEM)


def params():
    return pltpu.CompilerParams(vmem_limit_bytes=VMEM_BYTES)


def call(kernel, outs, *args, specs=None, scratch=(), cost=None, after=()):
    shapes = [jax.ShapeDtypeStruct(s, d) for s, d in outs]
    count = len(args)

    def run(*refs):
        kernel(*refs[:count], *refs[count + len(after) :])

    return pl.pallas_call(
        run,
        out_shape=shapes,
        in_specs=(specs or [full(a.shape) for a in args])
        + [pl.BlockSpec(memory_space=pl.ANY)] * len(after),
        out_specs=[full(s.shape) for s in shapes],
        scratch_shapes=scratch,
        compiler_params=params(),
        cost_estimate=cost,
    )(*args, *after)


def flat_index(spatial_count):
    return lax.axis_index("sample") * spatial_count + lax.axis_index("spatial")


def bit_of(value, bit):
    return lax.rem(lax.div(value, jnp.int32(1 << bit)), jnp.int32(2))


def sigmoid(value):
    return 1.0 / (1.0 + jnp.exp(-value))


def slope_of(value, sig):
    return sig * (1.0 + value * (1.0 - sig))


def dot(a, b, dims=((1,), (0,))):
    return lax.dot_general(a, b, (dims, ((), ())), preferred_element_type=f32)


def selection():
    row = lax.broadcasted_iota(jnp.int32, (144, 64), 0)
    col = lax.broadcasted_iota(jnp.int32, (144, 64), 1)
    pair, cell = lax.div(row, 16), lax.rem(row, 16)
    b, c = lax.div(pair, 3), lax.rem(pair, 3)
    k, j = lax.div(cell, 4), lax.rem(cell, 4)
    x, y = lax.div(col, 8), lax.rem(col, 8)
    hit = (x == 2 * k + c - 1) & (y == 2 * j + b - 1)
    return hit.astype(f32).astype(bf16)


def fill(vpad, x1, planes, first_hidden, count):
    for index, (e, plane) in enumerate(planes):
        vpad[index, :, 0:8, :] = jnp.zeros((8, 8, LANES), f32)
        for kt in range(8):
            vpad[index, kt, 8:24, :] = plane[:, kt * LANES : (kt + 1) * LANES].astype(f32)
    for index, (e, plane) in enumerate(planes):
        for b in range(3):
            tiles = [jnp.zeros((8, LANES), f32)]
            for kt in range(8):
                tiles.append(vpad[index, kt, pl.ds(7 + b, 8, stride=2), :])
            for kk in range(4):
                left = jnp.concatenate([tiles[2 * kk], tiles[2 * kk + 1]], 0).astype(bf16)
                right = jnp.concatenate([tiles[2 * kk + 1], tiles[2 * kk + 2]], 0).astype(bf16)
                for a in range(e % 2, 3, 2):
                    h = (e - a) // 2 - first_hidden
                    if 0 <= h < count:
                        rows = slice(h * 64 + kk * 16, h * 64 + kk * 16 + 16)
                        col = (a * 3 + b) * 256
                        x1[rows, col : col + LANES] = left
                        x1[rows, col + LANES : col + 2 * LANES] = right


def load_kernel(vol_hbm, w1_hbm, face, low, x1, w1p, vol, w1, vpad, sems):
    loads = [
        pltpu.make_async_copy(vol_hbm, vol, sems.at[0]),
        pltpu.make_async_copy(w1_hbm, w1, sems.at[1]),
    ]
    for load in loads:
        load.start()
    loads[0].wait()
    depth = vol.shape[0]
    face[...] = vol[depth - 3 : depth]
    low[...] = vol[0:2]
    planes = [(e, vol[e - 3]) for e in range(4, depth + 3)]
    fill(vpad, x1, planes, 2, x1.shape[0] // 64)
    loads[1].wait()
    for ab in range(9):
        w1p[ab * 256 : ab * 256 + 64, :] = jnp.zeros((64, 128), bf16)
        w1p[ab * 256 + 64 : (ab + 1) * 256, :] = w1[ab * 192 : (ab + 1) * 192, :]


def hidden_of(x1, w1p, slope, picked):
    first_pre = dot(x1[...], w1p[...])
    sig = sigmoid(first_pre)
    hidden = (first_pre * sig).astype(bf16)
    slope[...] = slope_of(first_pre, sig)
    select = selection()
    for h in range(hidden.shape[0] // 64):
        picked[h * 144 : (h + 1) * 144, :] = dot(
            select, hidden[h * 64 : (h + 1) * 64]
        ).astype(bf16)


def upper_kernel(x1, w1p, w2_hbm, cot_hbm, slope, picked, w2, cot, cot_in, sems):
    loads = [
        pltpu.make_async_copy(cot_hbm, cot_in, sems.at[0]),
        pltpu.make_async_copy(w2_hbm, w2, sems.at[1]),
    ]
    for load in loads:
        load.start()
    hidden_of(x1, w1p, slope, picked)
    loads[0].wait()
    row = lax.broadcasted_iota(jnp.int32, (16, 4), 0)
    col = lax.broadcasted_iota(jnp.int32, (16, 4), 1)
    for o in range(cot_in.shape[0]):
        cells = None
        for k in range(4):
            place = (row == 4 * k + col).astype(f32).astype(bf16)
            part = dot(place, cot_in[o, :, k * 256 : (k + 1) * 256])
            cells = part if cells is None else cells + part
        cot[o * 16 : (o + 1) * 16, :] = cells
    loads[1].wait()


def second_taps(x2, own_first, keep, send, first_tap, last_tap):
    columns = slice(first_tap * LANES, last_tap * LANES)
    rows = (last_tap - first_tap) * LANES
    grad = dot(x2[:, columns], own_first, ((0,), (0,)))
    keep[0:rows, :] = grad[:, :LANES]
    send[0:rows, :] = grad[:, LANES:].astype(bf16)


def clear(keep, send, start):
    if start < keep.shape[0]:
        keep[start:, :] = jnp.zeros((keep.shape[0] - start, LANES), f32)
        send[start:, :] = jnp.zeros((keep.shape[0] - start, LANES), bf16)


def lower_kernel(
    core_bit, spatial_count, halo, low, w1p, picked_up, w2, cot,
    keep, send, x1, slope, x2, d2, own_first, vpad, picked,
):
    inside = jnp.where(lax.axis_index("spatial") > 0, 1.0, 0.0).astype(f32)
    planes = [(e, halo[e].astype(f32) * inside) for e in range(3)]
    planes += [(e, low[e - 3]) for e in (3, 4)]
    fill(vpad, x1, planes, 0, 2)
    hidden_of(x1, w1p, slope, picked)
    out_planes = x2.shape[0] // 16
    for o in range(out_planes):
        for tap in range(27):
            h, pair = 2 * o + tap // 9, tap % 9
            if h < 2:
                cells = picked[h * 144 + pair * 16 : h * 144 + (pair + 1) * 16, :]
            else:
                at = (h - 2) * 144 + pair * 16
                cells = picked_up[at : at + 16, :]
            x2[o * 16 : (o + 1) * 16, tap * LANES : (tap + 1) * LANES] = cells
    second_pre = dot(x2[...], w2[...])
    sig = sigmoid(second_pre)
    delta = cot[...] * slope_of(second_pre, sig)
    d2[...] = delta.astype(bf16)
    core = bit_of(flat_index(spatial_count), core_bit)
    left, right = delta[:, :LANES], delta[:, LANES:]
    own_first[...] = jnp.concatenate(
        [jnp.where(core == 0, left, right), jnp.where(core == 0, right, left)], 1
    ).astype(bf16)
    second_taps(x2, own_first[...], keep, send, 0, SPLIT)
    clear(keep, send, SPLIT * LANES)


def last_kernel(
    core_bit, spatial_count, x1_up, x1_low, slope_up, slope_low, x2, d2, own_first, w2,
    keep, send, g1,
):
    second_taps(x2, own_first[...], keep, send, SPLIT, 27)
    out_planes = x2.shape[0] // 16
    hidden_planes = 2 * out_planes + 1
    select = selection()
    spread = dot(d2[...], w2[...], ((1,), (1,)))
    coarse = spread.astype(bf16)
    fine = (spread - coarse.astype(f32)).astype(bf16)
    deltas = []
    for h in range(hidden_planes):
        total = None
        for a in range(h % 2, 3, 2):
            o = (h - a) // 2
            if 0 <= o < out_planes:
                for piece in (coarse, fine):
                    stack = jnp.concatenate(
                        [
                            piece[o * 16 : (o + 1) * 16, tap * LANES : (tap + 1) * LANES]
                            for tap in range(a * 9, a * 9 + 9)
                        ],
                        0,
                    )
                    part = dot(select, stack, ((0,), (0,)))
                    total = part if total is None else total + part
        rounded = total.astype(bf16).astype(f32)
        if h < 2:
            slope = slope_low[h * 64 : (h + 1) * 64]
        else:
            slope = slope_up[(h - 2) * 64 : (h - 1) * 64]
        deltas.append((rounded * slope).astype(bf16))
    d1_low, d1_up = jnp.concatenate(deltas[:2], 0), jnp.concatenate(deltas[2:], 0)
    for a in range(3):
        columns = slice(a * 768, (a + 1) * 768)
        grad = dot(x1_up[:, columns], d1_up, ((0,), (0,)))
        grad = grad + dot(x1_low[:, columns], d1_low, ((0,), (0,)))
        for b in range(3):
            at = (a * 3 + b) * 192
            g1[at : at + 192, :] = grad[b * 256 + 64 : (b + 1) * 256]
    core = bit_of(flat_index(spatial_count), core_bit)
    start = (27 - SPLIT) * LANES
    mine = pl.ds(pl.multiple_of(core * FIRST, 8), FIRST)
    other = pl.ds(pl.multiple_of((1 - core) * FIRST, 8), FIRST)
    keep[start : start + FIRST, :] = g1[mine, :]
    send[start : start + FIRST, :] = g1[other, :].astype(bf16)
    clear(keep, send, start + FIRST)


def side_of(flat, orders, core, step):
    first, second = bit_of(flat, orders[0][step]), bit_of(flat, orders[1][step])
    return jnp.where(core == 0, first, second)


def reduce_kernel(orders, core_bit, step, spatial_count, keep, recv, kept, gone):
    half = keep.shape[0] // 2
    flat = flat_index(spatial_count)
    bit = side_of(flat, orders, bit_of(flat, core_bit), step)
    mine = pl.ds(pl.multiple_of(bit * half, 16), half)
    other = pl.ds(pl.multiple_of((1 - bit) * half, 16), half)
    kept[...] = keep[mine, :] + recv[mine, :].astype(f32)
    gone[...] = (keep[other, :] + recv[other, :].astype(f32)).astype(bf16)


def sum_kernel(keep, recv, out):
    out[...] = (keep[...].astype(f32) + recv[...].astype(f32)).astype(bf16)


def join_kernel(own, recv, out):
    half = own.shape[0]
    out[0:half, :] = own[...]
    out[half:, :] = recv[...]


def write_half(flat, side, orders, chunk, segments, part, wide, grad_first, grad_second, sems):
    steps = len(orders[0]) - 1
    bits = [side_of(flat, orders, side, s) for s in range(steps)]
    columns = pl.ds(pl.multiple_of(side * LANES, LANES), LANES)
    copies = []
    for place in range(1 << steps):
        position = jnp.int32(0)
        for s in range(steps):
            want = (place >> (steps - 1 - s)) & 1
            differs = (1 - bits[s]) if want else bits[s]
            position = position + differs * (1 << (steps - 1 - s))
        rows = pl.ds(pl.multiple_of(position * chunk, 16), chunk)
        at = place * chunk
        wide[at : at + chunk, :] = part[rows, :].astype(f32)
        for start, size, second, base in segments:
            low, high = max(start, at), min(start + size, at + chunk)
            if low >= high:
                continue
            to = base + low - start
            if second:
                target = grad_second.at[to : to + high - low, columns]
            else:
                target = grad_first.at[
                    pl.ds(pl.multiple_of(side * FIRST + to, 16), high - low)
                ]
            copy = pltpu.make_async_copy(wide.at[low:high], target, sems.at[len(copies)])
            copy.start()
            copies.append(copy)
    return copies


def final_kernel(core_bit, spatial_count, jobs, *refs):
    count = len(jobs)
    grad_first, grad_second = refs[-2 * count - 2 : -2 * count]
    wides, sems = refs[-2 * count : -count], refs[-count:]
    flat = flat_index(spatial_count)
    core = bit_of(flat, core_bit)
    copies = []
    for index, (own, orders, chunk, segments) in enumerate(jobs):
        side = core if own else 1 - core
        copies += write_half(
            flat, side, orders, chunk, segments,
            refs[index], wides[index], grad_first, grad_second, sems[index],
        )
    for copy in copies:
        copy.wait()


def body(spatial_count, sample_count, volume, w_first, w_second, cotangent):
    count = spatial_count * sample_count
    bits = count.bit_length() - 1
    core_bit = spatial_count.bit_length() - 1
    others = [bit for bit in range(bits) if bit != core_bit]
    turn, rest = others[:3], others[3:]
    orders = [
        [tuple(turn[i] for i in turns) + tuple(rest) for turns in lane] for lane in LANE_TURNS
    ]
    steps = len(others) - 1
    unit = 16 << steps
    second_rest = (27 - SPLIT) * LANES
    segments = [
        [(0, SPLIT * LANES, True, 0)],
        [(0, second_rest, True, SPLIT * LANES), (second_rest, FIRST, False, 0)],
    ]
    chunks = [-(-sum(seg[1] for seg in lane) // unit) * 16 for lane in segments]

    def swap_core(array):
        return lax.ppermute(array, BOTH, [(i, i ^ (1 << core_bit)) for i in range(count)])

    def swap(array, lane, step):
        pairs = [(i, i ^ (1 << orders[lane][(i >> core_bit) & 1][step])) for i in range(count)]
        return lax.ppermute(array, BOTH, pairs)

    slab = volume[0]
    depth = slab.shape[0]
    out_planes = depth // 4
    up = 2 * out_planes - 1
    slab_cot = cotangent[0]
    outside = pl.BlockSpec(memory_space=pl.ANY)
    far = pltpu.HBM
    face, low, x1_up, w1p = call(
        load_kernel,
        [
            ((3, 16, 1024), bf16),
            ((2, 16, 1024), bf16),
            ((up * 64, 9 * 256), bf16),
            ((9 * 256, 128), bf16),
        ],
        pltpu.with_memory_space_constraint(slab, far),
        pltpu.with_memory_space_constraint(w_first, far),
        specs=[outside, outside],
        scratch=[
            pltpu.VMEM(slab.shape, bf16),
            pltpu.VMEM(w_first.shape, bf16),
            pltpu.VMEM((depth - 1, 8, 24, LANES), f32),
            pltpu.SemaphoreType.DMA((2,)),
        ],
    )
    halo = lax.ppermute(
        face, "spatial", [(i, (i + 1) % spatial_count) for i in range(spatial_count)]
    )
    cells = out_planes * 16
    slope_up, picked_up, w2, cot = call(
        upper_kernel,
        [
            ((up * 64, LANES), f32),
            ((up * 144, LANES), bf16),
            (w_second.shape, bf16),
            ((cells, 256), f32),
        ],
        x1_up,
        w1p,
        pltpu.with_memory_space_constraint(w_second, far),
        pltpu.with_memory_space_constraint(slab_cot, far),
        specs=[full(None), full(None), outside, outside],
        scratch=[pltpu.VMEM(slab_cot.shape, bf16), pltpu.SemaphoreType.DMA((2,))],
        cost=pl.CostEstimate(flops=4 * 10**8, bytes_accessed=10**7, transcendentals=0),
    )
    rows = [chunk << steps for chunk in chunks]
    keep0, send0, x1_low, slope_low, x2, d2, own_first = call(
        functools.partial(lower_kernel, core_bit, spatial_count),
        [
            ((rows[0], LANES), f32),
            ((rows[0], LANES), bf16),
            ((128, 9 * 256), bf16),
            ((128, LANES), f32),
            ((cells, 27 * LANES), bf16),
            ((cells, 256), bf16),
            ((cells, 256), bf16),
        ],
        halo,
        low,
        w1p,
        picked_up,
        w2,
        cot,
        scratch=[pltpu.VMEM((5, 8, 24, LANES), f32), pltpu.VMEM((288, LANES), bf16)],
    )
    recv0 = swap_core(send0)
    keep1, send1 = call(
        functools.partial(last_kernel, core_bit, spatial_count),
        [((rows[1], LANES), f32), ((rows[1], LANES), bf16)],
        x1_up,
        x1_low,
        slope_up,
        slope_low,
        x2,
        d2,
        own_first,
        w2,
        scratch=[pltpu.VMEM((2 * FIRST, LANES), f32)],
        cost=pl.CostEstimate(flops=10**9, bytes_accessed=10**7, transcendentals=0),
    )
    recv1 = swap_core(send1)
    keep, recv, own = [keep0, keep1], [recv0, recv1], [None, None]
    last = send1
    for step in range(steps):
        for lane in range(2):
            half = keep[lane].shape[0] // 2
            keep[lane], last = call(
                functools.partial(reduce_kernel, orders[lane], core_bit, step, spatial_count),
                [((half, LANES), f32), ((half, LANES), bf16)],
                keep[lane],
                recv[lane],
                after=(last,),
                cost=STEP_COST,
            )
            recv[lane] = swap(last, lane, step)
    for turn in range(2):
        for lane in range(2):
            shape = [((chunks[lane], LANES), bf16)]
            last = call(sum_kernel, shape, keep[lane], recv[lane], after=(last,), cost=STEP_COST)[0]
            keep[lane], recv[lane] = last, swap(last, lane, steps - turn)
    for step in reversed(range(steps)):
        for lane in range(2):
            shape = [((2 * keep[lane].shape[0], LANES), bf16)]
            last = call(join_kernel, shape, keep[lane], recv[lane], after=(last,), cost=STEP_COST)[0]
            keep[lane] = last
            recv[lane] = swap(last, lane, step - 1) if step else swap_core(last)
    shapes = [jax.ShapeDtypeStruct((2 * FIRST, LANES), f32)]
    shapes += [jax.ShapeDtypeStruct((SECOND, 2 * LANES), f32)]
    grads = ()
    for group in (((0, True), (0, False), (1, True)), ((1, False),)):
        parts = [keep[lane] if mine else recv[lane] for lane, mine in group]
        jobs = [(mine, orders[lane], chunks[lane], segments[lane]) for lane, mine in group]
        grads = pl.pallas_call(
            functools.partial(final_kernel, core_bit, spatial_count, jobs),
            out_shape=shapes,
            in_specs=[full(part.shape) for part in parts] + [outside] * len(grads),
            out_specs=[outside] * 2,
            scratch_shapes=[pltpu.VMEM((rows[lane], LANES), f32) for lane, _ in group]
            + [pltpu.SemaphoreType.DMA(((1 << steps) + 1,)) for _ in group],
            input_output_aliases={len(parts): 0, len(parts) + 1: 1} if grads else {},
            compiler_params=params(),
        )(*parts, *grads)
    return grads


def solution(mesh):
    sizes = dict(mesh.shape)

    def run(*args):
        return tuple(body(sizes["spatial"], sizes["sample"], *args))

    return jax.shard_map(
        run,
        mesh=mesh,
        in_specs=(P("sample", "spatial", None, None), P(), P(), P("sample", "spatial", None, None)),
        out_specs=(P(), P()),
        check_vma=False,
    )
```

```python
import functools

import jax
import jax.numpy as jnp
from jax import lax
from jax.experimental import pallas as pl
from jax.experimental.pallas import tpu as pltpu
from jax.sharding import PartitionSpec as P

BOTH = ("sample", "spatial")
LANES = 128
SECOND, FIRST = 3456, 864
VMEM_BYTES = 32 * 1024 * 1024
SPLIT = 17
LANE_TURNS = (((0, 1, 2), (2, 0, 1)), ((1, 2, 0), (2, 0, 1)))
f32, bf16 = jnp.float32, jnp.bfloat16

WRITES = (((0, 0), (0, 2)), ((0, 1), (1, 0), (1, 2)), ((0, 3), (1, 1)), ((1, 3),))
STEP_COST = pl.CostEstimate(flops=4 * 10**9, bytes_accessed=8 * 10**7, transcendentals=0)


def full(shape):
    return pl.BlockSpec(memory_space=pltpu.VMEM)


def params():
    return pltpu.CompilerParams(vmem_limit_bytes=VMEM_BYTES)


def call(kernel, outs, *args, specs=None, scratch=(), cost=None, after=()):
    shapes = [jax.ShapeDtypeStruct(s, d) for s, d in outs]
    count = len(args)

    def run(*refs):
        kernel(*refs[:count], *refs[count + len(after) :])

    return pl.pallas_call(
        run,
        out_shape=shapes,
        in_specs=(specs or [full(a.shape) for a in args])
        + [pl.BlockSpec(memory_space=pl.ANY)] * len(after),
        out_specs=[full(s.shape) for s in shapes],
        scratch_shapes=scratch,
        compiler_params=params(),
        cost_estimate=cost,
    )(*args, *after)


def flat_index(spatial_count):
    return lax.axis_index("sample") * spatial_count + lax.axis_index("spatial")


def bit_of(value, bit):
    return lax.rem(lax.div(value, jnp.int32(1 << bit)), jnp.int32(2))


def half_of(flat, bits):
    total = jnp.int32(0)
    for bit in range(bits):
        total = total + bit_of(flat, bit)
    return lax.rem(total, jnp.int32(2))


def sigmoid(value):
    return 1.0 / (1.0 + jnp.exp(-value))


def slope_of(value, sig):
    return sig * (1.0 + value * (1.0 - sig))


def dot(a, b, dims=((1,), (0,))):
    return lax.dot_general(a, b, (dims, ((), ())), preferred_element_type=f32)


def selection():
    row = lax.broadcasted_iota(jnp.int32, (144, 64), 0)
    col = lax.broadcasted_iota(jnp.int32, (144, 64), 1)
    pair, cell = lax.div(row, 16), lax.rem(row, 16)
    b, c = lax.div(pair, 3), lax.rem(pair, 3)
    k, j = lax.div(cell, 4), lax.rem(cell, 4)
    x, y = lax.div(col, 8), lax.rem(col, 8)
    hit = (x == 2 * k + c - 1) & (y == 2 * j + b - 1)
    return hit.astype(f32).astype(bf16)


def fill(vpad, x1, planes, first_hidden, count):
    for index, (e, plane) in enumerate(planes):
        vpad[index, :, 0:8, :] = jnp.zeros((8, 8, LANES), f32)
        for kt in range(8):
            vpad[index, kt, 8:24, :] = plane[:, kt * LANES : (kt + 1) * LANES].astype(f32)
    for index, (e, plane) in enumerate(planes):
        for b in range(3):
            tiles = [jnp.zeros((8, LANES), f32)]
            for kt in range(8):
                tiles.append(vpad[index, kt, pl.ds(7 + b, 8, stride=2), :])
            for kk in range(4):
                left = jnp.concatenate([tiles[2 * kk], tiles[2 * kk + 1]], 0).astype(bf16)
                right = jnp.concatenate([tiles[2 * kk + 1], tiles[2 * kk + 2]], 0).astype(bf16)
                for a in range(e % 2, 3, 2):
                    h = (e - a) // 2 - first_hidden
                    if 0 <= h < count:
                        rows = slice(h * 64 + kk * 16, h * 64 + kk * 16 + 16)
                        col = (a * 3 + b) * 256
                        x1[rows, col : col + LANES] = left
                        x1[rows, col + LANES : col + 2 * LANES] = right


def load_kernel(vol_hbm, w1_hbm, face, low, x1, w1p, vol, w1, vpad, sems):
    loads = [
        pltpu.make_async_copy(vol_hbm, vol, sems.at[0]),
        pltpu.make_async_copy(w1_hbm, w1, sems.at[1]),
    ]
    for load in loads:
        load.start()
    loads[0].wait()
    depth = vol.shape[0]
    face[...] = vol[depth - 3 : depth]
    low[...] = vol[0:2]
    planes = [(e, vol[e - 3]) for e in range(4, depth + 3)]
    fill(vpad, x1, planes, 2, x1.shape[0] // 64)
    loads[1].wait()
    for ab in range(9):
        w1p[ab * 256 : ab * 256 + 64, :] = jnp.zeros((64, 128), bf16)
        w1p[ab * 256 + 64 : (ab + 1) * 256, :] = w1[ab * 192 : (ab + 1) * 192, :]


def hidden_of(x1, w1p, slope, picked):
    first_pre = dot(x1[...], w1p[...])
    sig = sigmoid(first_pre)
    hidden = (first_pre * sig).astype(bf16)
    slope[...] = slope_of(first_pre, sig)
    select = selection()
    for h in range(hidden.shape[0] // 64):
        picked[h * 144 : (h + 1) * 144, :] = dot(
            select, hidden[h * 64 : (h + 1) * 64]
        ).astype(bf16)


def upper_kernel(x1, w1p, w2_hbm, cot_hbm, slope, picked, w2, cot, cot_in, sems):
    loads = [
        pltpu.make_async_copy(cot_hbm, cot_in, sems.at[0]),
        pltpu.make_async_copy(w2_hbm, w2, sems.at[1]),
    ]
    for load in loads:
        load.start()
    hidden_of(x1, w1p, slope, picked)
    loads[0].wait()
    row = lax.broadcasted_iota(jnp.int32, (16, 4), 0)
    col = lax.broadcasted_iota(jnp.int32, (16, 4), 1)
    for o in range(cot_in.shape[0]):
        cells = None
        for k in range(4):
            place = (row == 4 * k + col).astype(f32).astype(bf16)
            part = dot(place, cot_in[o, :, k * 256 : (k + 1) * 256])
            cells = part if cells is None else cells + part
        cot[o * 16 : (o + 1) * 16, :] = cells
    loads[1].wait()


def second_taps(x2, own_first, keep, send, first_tap, last_tap):
    columns = slice(first_tap * LANES, last_tap * LANES)
    rows = (last_tap - first_tap) * LANES // 2
    half = keep.shape[0] // 2
    grad = dot(x2[:, columns], own_first, ((0,), (0,)))
    for v in range(2):
        keep[v * half : v * half + rows, :] = grad[v * rows : (v + 1) * rows, :LANES]
        send[v * half : v * half + rows, :] = grad[v * rows : (v + 1) * rows, LANES:].astype(bf16)


def clear(keep, send, start):
    half = keep.shape[0] // 2
    if start < half:
        for v in range(2):
            rows = slice(v * half + start, (v + 1) * half)
            keep[rows, :] = jnp.zeros((half - start, LANES), f32)
            send[rows, :] = jnp.zeros((half - start, LANES), bf16)


def lower_kernel(
    bits, spatial_count, halo, low, w1p, picked_up, w2, cot,
    keep, send, x1, slope, x2, d2, own_first, vpad, picked,
):
    inside = jnp.where(lax.axis_index("spatial") > 0, 1.0, 0.0).astype(f32)
    planes = [(e, halo[e].astype(f32) * inside) for e in range(3)]
    planes += [(e, low[e - 3]) for e in (3, 4)]
    fill(vpad, x1, planes, 0, 2)
    hidden_of(x1, w1p, slope, picked)
    out_planes = x2.shape[0] // 16
    for o in range(out_planes):
        for tap in range(27):
            h, pair = 2 * o + tap // 9, tap % 9
            if h < 2:
                cells = picked[h * 144 + pair * 16 : h * 144 + (pair + 1) * 16, :]
            else:
                at = (h - 2) * 144 + pair * 16
                cells = picked_up[at : at + 16, :]
            x2[o * 16 : (o + 1) * 16, tap * LANES : (tap + 1) * LANES] = cells
    second_pre = dot(x2[...], w2[...])
    sig = sigmoid(second_pre)
    delta = cot[...] * slope_of(second_pre, sig)
    d2[...] = delta.astype(bf16)
    core = half_of(flat_index(spatial_count), bits)
    left, right = delta[:, :LANES], delta[:, LANES:]
    own_first[...] = jnp.concatenate(
        [jnp.where(core == 0, left, right), jnp.where(core == 0, right, left)], 1
    ).astype(bf16)
    second_taps(x2, own_first[...], keep, send, 0, SPLIT)
    clear(keep, send, SPLIT * LANES // 2)


def last_kernel(
    bits, spatial_count, x1_up, x1_low, slope_up, slope_low, x2, d2, own_first, w2,
    keep, send, g1,
):
    second_taps(x2, own_first[...], keep, send, SPLIT, 27)
    out_planes = x2.shape[0] // 16
    hidden_planes = 2 * out_planes + 1
    select = selection()
    spread = dot(d2[...], w2[...], ((1,), (1,)))
    coarse = spread.astype(bf16)
    fine = (spread - coarse.astype(f32)).astype(bf16)
    deltas = []
    for h in range(hidden_planes):
        total = None
        for a in range(h % 2, 3, 2):
            o = (h - a) // 2
            if 0 <= o < out_planes:
                for piece in (coarse, fine):
                    stack = jnp.concatenate(
                        [
                            piece[o * 16 : (o + 1) * 16, tap * LANES : (tap + 1) * LANES]
                            for tap in range(a * 9, a * 9 + 9)
                        ],
                        0,
                    )
                    part = dot(select, stack, ((0,), (0,)))
                    total = part if total is None else total + part
        rounded = total.astype(bf16).astype(f32)
        if h < 2:
            slope = slope_low[h * 64 : (h + 1) * 64]
        else:
            slope = slope_up[(h - 2) * 64 : (h - 1) * 64]
        deltas.append((rounded * slope).astype(bf16))
    d1_low, d1_up = jnp.concatenate(deltas[:2], 0), jnp.concatenate(deltas[2:], 0)
    for a in range(3):
        columns = slice(a * 768, (a + 1) * 768)
        grad = dot(x1_up[:, columns], d1_up, ((0,), (0,)))
        grad = grad + dot(x1_low[:, columns], d1_low, ((0,), (0,)))
        for b in range(3):
            at = (a * 3 + b) * 192
            g1[at : at + 192, :] = grad[b * 256 + 64 : (b + 1) * 256]
    core = half_of(flat_index(spatial_count), bits)
    start, quarter = (27 - SPLIT) * LANES // 2, FIRST // 2
    for v in range(2):
        rows = slice(v * (keep.shape[0] // 2) + start, v * (keep.shape[0] // 2) + start + quarter)
        mine = pl.ds(pl.multiple_of(core * FIRST + v * quarter, 8), quarter)
        other = pl.ds(pl.multiple_of((1 - core) * FIRST + v * quarter, 8), quarter)
        keep[rows, :] = g1[mine, :]
        send[rows, :] = g1[other, :].astype(bf16)
    clear(keep, send, start + quarter)


def side_of(flat, orders, core, step):
    first, second = bit_of(flat, orders[0][step]), bit_of(flat, orders[1][step])
    return jnp.where(core == 0, first, second)


def reduce_kernel(orders, bits, step, spatial_count, keep, recv, kept, gone):
    half = keep.shape[0] // 2
    flat = flat_index(spatial_count)
    bit = side_of(flat, orders, half_of(flat, bits), step)
    mine = pl.ds(pl.multiple_of(bit * half, 16), half)
    other = pl.ds(pl.multiple_of((1 - bit) * half, 16), half)
    kept[...] = keep[mine, :] + recv[mine, :].astype(f32)
    gone[...] = (keep[other, :] + recv[other, :].astype(f32)).astype(bf16)


def sum_kernel(keep, recv, out):
    out[...] = (keep[...].astype(f32) + recv[...].astype(f32)).astype(bf16)


def join_kernel(own, recv, out):
    half = own.shape[0]
    out[0:half, :] = own[...]
    out[half:, :] = recv[...]


def copy_kernel(got, out):
    out[...] = got[...]


def start_part(flat, side, orders, chunk, segments, last, part, wide, grad_first, grad_second, sems):
    steps = len(orders[0]) - 1
    bits = [side_of(flat, orders, side, s) for s in range(steps)]
    columns = pl.ds(pl.multiple_of(side * LANES, LANES), LANES)
    top = 1 - bits[0] if last else bits[0]
    copies = []
    for place in range(1 << (steps - 1)):
        position = jnp.int32(0)
        for s in range(1, steps):
            want = (place >> (steps - 1 - s)) & 1
            differs = (1 - bits[s]) if want else bits[s]
            position = position + differs * (1 << (steps - 1 - s))
        at = place * chunk
        rows = pl.ds(pl.multiple_of(position * chunk, 16), chunk)
        wide[at : at + chunk, :] = part[rows, :].astype(f32)
        for start, size, second, base in segments:
            low, high = max(start, at), min(start + size, at + chunk)
            if low >= high:
                continue
            to = top * size + base + low - start
            if second:
                target = grad_second.at[pl.ds(pl.multiple_of(to, 16), high - low), columns]
            else:
                to = pl.multiple_of(side * FIRST + to, 16)
                target = grad_first.at[pl.ds(to, high - low)]
            copy = pltpu.make_async_copy(wide.at[low:high], target, sems.at[len(copies)])
            copy.start()
            copies.append(copy)
    return copies


def final_kernel(bits, spatial_count, jobs, chained, *refs):
    count = len(jobs)
    tokens = refs[count + 2 * chained + 2 : -2 * count]
    grad_first, grad_second = refs[count + 2 * chained : count + 2 * chained + 2]
    wides, sems = refs[-2 * count : -count], refs[-count:]
    flat = flat_index(spatial_count)
    core = half_of(flat, bits)
    for token in tokens:
        token[...] = jnp.zeros(token.shape, f32)
    copies = []
    for index, (own, orders, chunk, segments, last) in enumerate(jobs):
        copies += start_part(
            flat, core if own else 1 - core, orders, chunk, segments, last,
            refs[index], wides[index], grad_first, grad_second, sems[index],
        )
    for copy in copies:
        copy.wait()


def body(spatial_count, sample_count, volume, w_first, w_second, cotangent):
    count = spatial_count * sample_count
    bits = count.bit_length() - 1
    core_bit = spatial_count.bit_length() - 1
    others = [bit for bit in range(bits) if bit != core_bit]
    turn, rest = others[:3], others[3:]
    orders = [
        [tuple(turn[i] for i in turns) + tuple(rest) for turns in lane] for lane in LANE_TURNS
    ]
    steps = len(others) - 1
    lanes = len(LANE_TURNS)
    unit = 16 << steps
    second_rest = (27 - SPLIT) * LANES // 2
    segments = [
        [(0, SPLIT * LANES // 2, True, 0)],
        [(0, second_rest, True, SPLIT * LANES), (second_rest, FIRST // 2, False, 0)],
    ]
    chunks = [-(-2 * sum(seg[1] for seg in lane) // unit) * 16 for lane in segments]

    def swap_core(array):
        return lax.ppermute(array, BOTH, [(i, i ^ (1 << core_bit)) for i in range(count)])

    def swap(array, lane, step):
        pairs = []
        for i in range(count):
            bit = orders[lane][i.bit_count() % 2][step]
            pairs.append((i, i ^ (1 << bit) ^ (1 << core_bit)))
        return lax.ppermute(array, BOTH, pairs)

    slab = volume[0]
    depth = slab.shape[0]
    out_planes = depth // 4
    up = 2 * out_planes - 1
    slab_cot = cotangent[0]
    outside = pl.BlockSpec(memory_space=pl.ANY)
    far = pltpu.HBM
    face, low, x1_up, w1p = call(
        load_kernel,
        [
            ((3, 16, 1024), bf16),
            ((2, 16, 1024), bf16),
            ((up * 64, 9 * 256), bf16),
            ((9 * 256, 128), bf16),
        ],
        pltpu.with_memory_space_constraint(slab, far),
        pltpu.with_memory_space_constraint(w_first, far),
        specs=[outside, outside],
        scratch=[
            pltpu.VMEM(slab.shape, bf16),
            pltpu.VMEM(w_first.shape, bf16),
            pltpu.VMEM((depth - 1, 8, 24, LANES), f32),
            pltpu.SemaphoreType.DMA((2,)),
        ],
    )
    halo = lax.ppermute(
        face, "spatial", [(i, (i + 1) % spatial_count) for i in range(spatial_count)]
    )
    cells = out_planes * 16
    slope_up, picked_up, w2, cot = call(
        upper_kernel,
        [
            ((up * 64, LANES), f32),
            ((up * 144, LANES), bf16),
            (w_second.shape, bf16),
            ((cells, 256), f32),
        ],
        x1_up,
        w1p,
        pltpu.with_memory_space_constraint(w_second, far),
        pltpu.with_memory_space_constraint(slab_cot, far),
        specs=[full(None), full(None), outside, outside],
        scratch=[pltpu.VMEM(slab_cot.shape, bf16), pltpu.SemaphoreType.DMA((2,))],
        cost=pl.CostEstimate(flops=4 * 10**8, bytes_accessed=10**7, transcendentals=0),
    )
    rows = [chunk << steps for chunk in chunks]
    keep0, send0, x1_low, slope_low, x2, d2, own_first = call(
        functools.partial(lower_kernel, bits, spatial_count),
        [
            ((rows[0], LANES), f32),
            ((rows[0], LANES), bf16),
            ((128, 9 * 256), bf16),
            ((128, LANES), f32),
            ((cells, 27 * LANES), bf16),
            ((cells, 256), bf16),
            ((cells, 256), bf16),
        ],
        halo,
        low,
        w1p,
        picked_up,
        w2,
        cot,
        scratch=[pltpu.VMEM((5, 8, 24, LANES), f32), pltpu.VMEM((288, LANES), bf16)],
    )
    recv0 = swap_core(send0)
    keep1, send1 = call(
        functools.partial(last_kernel, bits, spatial_count),
        [((rows[1], LANES), f32), ((rows[1], LANES), bf16)],
        x1_up,
        x1_low,
        slope_up,
        slope_low,
        x2,
        d2,
        own_first,
        w2,
        scratch=[pltpu.VMEM((2 * FIRST, LANES), f32)],
        cost=pl.CostEstimate(flops=10**9, bytes_accessed=10**7, transcendentals=0),
    )
    recv1 = swap_core(send1)
    keep, recv = [keep0, keep1], [recv0, recv1]
    last = send1
    for step in range(steps):
        for lane in range(lanes):
            half = keep[lane].shape[0] // 2
            keep[lane], last = call(
                functools.partial(reduce_kernel, orders[lane], bits, step, spatial_count),
                [((half, LANES), f32), ((half, LANES), bf16)],
                keep[lane],
                recv[lane],
                after=(last,),
                cost=STEP_COST,
            )
            recv[lane] = swap(last, lane, step)
    for turn in range(2):
        for lane in range(lanes):
            shape = [((chunks[lane], LANES), bf16)]
            last = call(sum_kernel, shape, keep[lane], recv[lane], after=(last,), cost=STEP_COST)[0]
            keep[lane], recv[lane] = last, swap(last, lane, steps - turn)
    for step in reversed(range(1, steps)):
        for lane in range(lanes):
            shape = [((2 * keep[lane].shape[0], LANES), bf16)]
            last = call(
                join_kernel, shape, keep[lane], recv[lane], after=(last,), cost=STEP_COST
            )[0]
            keep[lane], recv[lane] = last, swap(last, lane, step - 1)
    held = [[keep[lane], None, swap_core(keep[lane]), None] for lane in range(lanes)]
    shapes = [jax.ShapeDtypeStruct((2 * FIRST, LANES), f32)]
    shapes += [jax.ShapeDtypeStruct((SECOND, 2 * LANES), f32)]
    token_shape = [jax.ShapeDtypeStruct((8, LANES), f32)]
    grads = []

    def write(group, grads, token):
        parts = [held[lane][which] for lane, which in group]
        jobs = [
            (which < 2, orders[lane], chunks[lane], segments[lane], which % 2 == 1)
            for lane, which in group
        ]
        return pl.pallas_call(
            functools.partial(final_kernel, bits, spatial_count, jobs, bool(grads)),
            out_shape=shapes + token_shape * token,
            in_specs=[full(part.shape) for part in parts] + [outside] * len(grads),
            out_specs=[outside] * 2 + [full(None)] * token,
            scratch_shapes=[pltpu.VMEM((rows[lane] // 2, LANES), f32) for lane, _ in group]
            + [pltpu.SemaphoreType.DMA(((1 << steps) + 1,)) for _ in group],
            input_output_aliases={len(parts): 0, len(parts) + 1: 1} if grads else {},
            compiler_params=params(),
            cost_estimate=STEP_COST,
        )(*parts, *grads)

    for lane, group in enumerate(WRITES[:lanes]):
        *grads, token = write(group, grads, 1)
        shape = [(recv[lane].shape, bf16)]
        last = call(copy_kernel, shape, recv[lane], after=(last, token), cost=STEP_COST)[0]
        held[lane][1], held[lane][3] = last, swap_core(last)
    for group in WRITES[lanes:]:
        grads = write(group, grads, 0)
    return grads


def solution(mesh):
    sizes = dict(mesh.shape)

    def run(*args):
        return tuple(body(sizes["spatial"], sizes["sample"], *args))

    return jax.shard_map(
        run,
        mesh=mesh,
        in_specs=(P("sample", "spatial", None, None), P(), P(), P("sample", "spatial", None, None)),
        out_specs=(P(), P()),
        check_vma=False,
    )
```

```python
import functools

import jax
import jax.numpy as jnp
from jax import lax
from jax.experimental import pallas as pl
from jax.experimental.pallas import tpu as pltpu
from jax.sharding import PartitionSpec as P

BOTH = ("sample", "spatial")
LANES = 128
SECOND, FIRST = 3456, 864
VMEM_BYTES = 32 * 1024 * 1024
SPLIT = 17
LANE_TURNS = (((0, 1, 2), (1, 2, 0)), ((2, 0, 1), (1, 2, 0)))
f32, bf16 = jnp.float32, jnp.bfloat16

WRITES = (((0, 0), (0, 2)), ((0, 1), (1, 0), (1, 2)), ((0, 3), (1, 1)), ((1, 3),))
STEP_COST = pl.CostEstimate(flops=4 * 10**9, bytes_accessed=8 * 10**7, transcendentals=0)


def full(shape):
    return pl.BlockSpec(memory_space=pltpu.VMEM)


def params():
    return pltpu.CompilerParams(vmem_limit_bytes=VMEM_BYTES)


def call(kernel, outs, *args, specs=None, scratch=(), cost=None, after=()):
    shapes = [jax.ShapeDtypeStruct(s, d) for s, d in outs]
    count = len(args)

    def run(*refs):
        kernel(*refs[:count], *refs[count + len(after) :])

    return pl.pallas_call(
        run,
        out_shape=shapes,
        in_specs=(specs or [full(a.shape) for a in args])
        + [pl.BlockSpec(memory_space=pl.ANY)] * len(after),
        out_specs=[full(s.shape) for s in shapes],
        scratch_shapes=scratch,
        compiler_params=params(),
        cost_estimate=cost,
    )(*args, *after)


def flat_index(spatial_count):
    return lax.axis_index("sample") * spatial_count + lax.axis_index("spatial")


def bit_of(value, bit):
    return lax.rem(lax.div(value, jnp.int32(1 << bit)), jnp.int32(2))


def half_of(flat, bits):
    total = jnp.int32(0)
    for bit in range(bits):
        total = total + bit_of(flat, bit)
    return lax.rem(total, jnp.int32(2))


def sigmoid(value):
    return 1.0 / (1.0 + jnp.exp(-value))


def slope_of(value, sig):
    return sig * (1.0 + value * (1.0 - sig))


def dot(a, b, dims=((1,), (0,))):
    return lax.dot_general(a, b, (dims, ((), ())), preferred_element_type=f32)


def selection():
    row = lax.broadcasted_iota(jnp.int32, (144, 64), 0)
    col = lax.broadcasted_iota(jnp.int32, (144, 64), 1)
    pair, cell = lax.div(row, 16), lax.rem(row, 16)
    b, c = lax.div(pair, 3), lax.rem(pair, 3)
    k, j = lax.div(cell, 4), lax.rem(cell, 4)
    x, y = lax.div(col, 8), lax.rem(col, 8)
    hit = (x == 2 * k + c - 1) & (y == 2 * j + b - 1)
    return hit.astype(f32).astype(bf16)


def fill(vpad, x1, planes, first_hidden, count):
    for index, (e, plane) in enumerate(planes):
        vpad[index, :, 0:8, :] = jnp.zeros((8, 8, LANES), f32)
        for kt in range(8):
            vpad[index, kt, 8:24, :] = plane[:, kt * LANES : (kt + 1) * LANES].astype(f32)
    for index, (e, plane) in enumerate(planes):
        for b in range(3):
            tiles = [jnp.zeros((8, LANES), f32)]
            for kt in range(8):
                tiles.append(vpad[index, kt, pl.ds(7 + b, 8, stride=2), :])
            for kk in range(4):
                left = jnp.concatenate([tiles[2 * kk], tiles[2 * kk + 1]], 0).astype(bf16)
                right = jnp.concatenate([tiles[2 * kk + 1], tiles[2 * kk + 2]], 0).astype(bf16)
                for a in range(e % 2, 3, 2):
                    h = (e - a) // 2 - first_hidden
                    if 0 <= h < count:
                        rows = slice(h * 64 + kk * 16, h * 64 + kk * 16 + 16)
                        col = (a * 3 + b) * 256
                        x1[rows, col : col + LANES] = left
                        x1[rows, col + LANES : col + 2 * LANES] = right


def load_kernel(vol_hbm, w1_hbm, x1_mid, x1, w1p, vol, w1, vpad, sems):
    loads = [
        pltpu.make_async_copy(vol_hbm, vol, sems.at[0]),
        pltpu.make_async_copy(w1_hbm, w1, sems.at[1]),
    ]
    for load in loads:
        load.start()
    loads[0].wait()
    depth = vol.shape[0]
    fill(vpad, x1_mid, [(e, vol[e - 3]) for e in (3, 4)], 1, 1)
    planes = [(e, vol[e - 3]) for e in range(4, depth + 3)]
    fill(vpad, x1, planes, 2, x1.shape[0] // 64)
    loads[1].wait()
    for ab in range(9):
        w1p[ab * 256 : ab * 256 + 64, :] = jnp.zeros((64, 128), bf16)
        w1p[ab * 256 + 64 : (ab + 1) * 256, :] = w1[ab * 192 : (ab + 1) * 192, :]


def hidden_of(x1, w1p, slope, picked):
    first_pre = dot(x1[...], w1p[...])
    sig = sigmoid(first_pre)
    hidden = (first_pre * sig).astype(bf16)
    slope[...] = slope_of(first_pre, sig)
    select = selection()
    planes = hidden.shape[0] // 64
    for h in range(0, planes, 2):
        pair = [hidden[g * 64 : (g + 1) * 64] for g in range(h, min(h + 2, planes))]
        cells = dot(select, jnp.concatenate(pair, 1)).astype(bf16)
        for g in range(len(pair)):
            at = (h + g) * 144
            picked[at : at + 144, :] = cells[:, g * LANES : (g + 1) * LANES]


def upper_kernel(x1, w1p, cot_hbm, slope, picked, cot, cot_in, sems):
    loads = [
        pltpu.make_async_copy(cot_hbm, cot_in, sems.at[0]),
    ]
    for load in loads:
        load.start()
    hidden_of(x1, w1p, slope, picked)
    loads[0].wait()
    row = lax.broadcasted_iota(jnp.int32, (16, 4), 0)
    col = lax.broadcasted_iota(jnp.int32, (16, 4), 1)
    for o in range(cot_in.shape[0]):
        cells = None
        for k in range(4):
            place = (row == 4 * k + col).astype(f32).astype(bf16)
            part = dot(place, cot_in[o, :, k * 256 : (k + 1) * 256])
            cells = part if cells is None else cells + part
        cot[o * 16 : (o + 1) * 16, :] = cells


def second_taps(x2, own_first, keep, send, first_tap, last_tap):
    columns = slice(first_tap * LANES, last_tap * LANES)
    rows = (last_tap - first_tap) * LANES // 2
    half = keep.shape[0] // 2
    grad = dot(x2[:, columns], own_first, ((0,), (0,)))
    for v in range(2):
        keep[v * half : v * half + rows, :] = grad[v * rows : (v + 1) * rows, :LANES]
        send[v * half : v * half + rows, :] = grad[v * rows : (v + 1) * rows, LANES:].astype(bf16)


def clear(keep, send, start):
    half = keep.shape[0] // 2
    if start < half:
        for v in range(2):
            rows = slice(v * half + start, (v + 1) * half)
            keep[rows, :] = jnp.zeros((half - start, LANES), f32)
            send[rows, :] = jnp.zeros((half - start, LANES), bf16)


def lower_kernel(
    bits, spatial_count, halo, x1_mid, w1p, picked_up, w2, cot,
    keep, send, x1, slope, x2, d2, own_first, vpad, picked,
):
    inside = jnp.where(lax.axis_index("spatial") > 0, 1.0, 0.0).astype(f32)
    planes = [(e, halo[e].astype(f32) * inside) for e in range(3)]
    fill(vpad, x1, planes, 0, 2)
    x1[64:128, 768:] = x1_mid[:, 768:]
    hidden_of(x1, w1p, slope, picked)
    out_planes = x2.shape[0] // 16
    for o in range(out_planes):
        for tap in range(27):
            h, pair = 2 * o + tap // 9, tap % 9
            if h < 2:
                cells = picked[h * 144 + pair * 16 : h * 144 + (pair + 1) * 16, :]
            else:
                at = (h - 2) * 144 + pair * 16
                cells = picked_up[at : at + 16, :]
            x2[o * 16 : (o + 1) * 16, tap * LANES : (tap + 1) * LANES] = cells
    second_pre = dot(x2[...], w2[...])
    sig = sigmoid(second_pre)
    delta = cot[...] * slope_of(second_pre, sig)
    d2[...] = delta.astype(bf16)
    core = half_of(flat_index(spatial_count), bits)
    left, right = delta[:, :LANES], delta[:, LANES:]
    own_first[...] = jnp.concatenate(
        [jnp.where(core == 0, left, right), jnp.where(core == 0, right, left)], 1
    ).astype(bf16)
    second_taps(x2, own_first[...], keep, send, 0, SPLIT)
    clear(keep, send, SPLIT * LANES // 2)


def last_kernel(
    bits, spatial_count, x1_up, x1_low, slope_up, slope_low, x2, d2, own_first, w2,
    keep, send, g1,
):
    second_taps(x2, own_first[...], keep, send, SPLIT, 27)
    out_planes = x2.shape[0] // 16
    hidden_planes = 2 * out_planes + 1
    select = selection()
    spread = dot(d2[...], w2[...], ((1,), (1,)))
    coarse = spread.astype(bf16)
    fine = (spread - coarse.astype(f32)).astype(bf16)
    deltas = []
    for h in range(hidden_planes):
        total = None
        for a in range(h % 2, 3, 2):
            o = (h - a) // 2
            if 0 <= o < out_planes:
                rows = slice(o * 16, (o + 1) * 16)
                stack = []
                for tap in range(a * 9, a * 9 + 9):
                    columns = slice(tap * LANES, (tap + 1) * LANES)
                    stack.append(jnp.concatenate([coarse[rows, columns], fine[rows, columns]], 1))
                both = dot(select, jnp.concatenate(stack, 0), ((0,), (0,)))
                part = both[:, :LANES] + both[:, LANES:]
                total = part if total is None else total + part
        rounded = total.astype(bf16).astype(f32)
        if h < 2:
            slope = slope_low[h * 64 : (h + 1) * 64]
        else:
            slope = slope_up[(h - 2) * 64 : (h - 1) * 64]
        deltas.append((rounded * slope).astype(bf16))
    d1_low, d1_up = jnp.concatenate(deltas[:2], 0), jnp.concatenate(deltas[2:], 0)
    for a in range(3):
        columns = slice(a * 768, (a + 1) * 768)
        grad = dot(d1_up, x1_up[:, columns], ((0,), (0,)))
        grad = (grad + dot(d1_low, x1_low[:, columns], ((0,), (0,)))).T
        for b in range(3):
            at = (a * 3 + b) * 192
            g1[at : at + 192, :] = grad[b * 256 + 64 : (b + 1) * 256]
    core = half_of(flat_index(spatial_count), bits)
    start, quarter = (27 - SPLIT) * LANES // 2, FIRST // 2
    for v in range(2):
        rows = slice(v * (keep.shape[0] // 2) + start, v * (keep.shape[0] // 2) + start + quarter)
        mine = pl.ds(pl.multiple_of(core * FIRST + v * quarter, 8), quarter)
        other = pl.ds(pl.multiple_of((1 - core) * FIRST + v * quarter, 8), quarter)
        keep[rows, :] = g1[mine, :]
        send[rows, :] = g1[other, :].astype(bf16)
    clear(keep, send, start + quarter)


def side_of(flat, orders, core, step):
    first, second = bit_of(flat, orders[0][step]), bit_of(flat, orders[1][step])
    return jnp.where(core == 0, first, second)


def reduce_kernel(orders, bits, step, spatial_count, keep, recv, kept, gone):
    half = keep.shape[0] // 2
    flat = flat_index(spatial_count)
    bit = side_of(flat, orders, half_of(flat, bits), step)
    mine = pl.ds(pl.multiple_of(bit * half, 16), half)
    other = pl.ds(pl.multiple_of((1 - bit) * half, 16), half)
    kept[...] = keep[mine, :] + recv[mine, :].astype(f32)
    gone[...] = (keep[other, :] + recv[other, :].astype(f32)).astype(bf16)


def sum_kernel(keep, recv, out):
    out[...] = (keep[...].astype(f32) + recv[...].astype(f32)).astype(bf16)


def join_kernel(own, recv, out):
    half = own.shape[0]
    out[0:half, :] = own[...]
    out[half:, :] = recv[...]


def copy_kernel(got, out):
    out[...] = got[...]


def start_part(flat, side, orders, chunk, segments, last, part, wide, grad_first, grad_second, sems):
    steps = len(orders[0]) - 1
    bits = [side_of(flat, orders, side, s) for s in range(steps)]
    columns = pl.ds(pl.multiple_of(side * LANES, LANES), LANES)
    top = 1 - bits[0] if last else bits[0]
    copies = []
    for place in range(1 << (steps - 1)):
        position = jnp.int32(0)
        for s in range(1, steps):
            want = (place >> (steps - 1 - s)) & 1
            differs = (1 - bits[s]) if want else bits[s]
            position = position + differs * (1 << (steps - 1 - s))
        at = place * chunk
        rows = pl.ds(pl.multiple_of(position * chunk, 16), chunk)
        wide[at : at + chunk, :] = part[rows, :].astype(f32)
        for start, size, second, base in segments:
            low, high = max(start, at), min(start + size, at + chunk)
            if low >= high:
                continue
            to = top * size + base + low - start
            if second:
                target = grad_second.at[pl.ds(pl.multiple_of(to, 16), high - low), columns]
            else:
                to = pl.multiple_of(side * FIRST + to, 16)
                target = grad_first.at[pl.ds(to, high - low)]
            copy = pltpu.make_async_copy(wide.at[low:high], target, sems.at[len(copies)])
            copy.start()
            copies.append(copy)
    return copies


def final_kernel(bits, spatial_count, jobs, chained, *refs):
    count = len(jobs)
    tokens = refs[count + 2 * chained + 2 : -2 * count]
    grad_first, grad_second = refs[count + 2 * chained : count + 2 * chained + 2]
    wides, sems = refs[-2 * count : -count], refs[-count:]
    flat = flat_index(spatial_count)
    core = half_of(flat, bits)
    for token in tokens:
        token[...] = jnp.zeros(token.shape, f32)
    copies = []
    for index, (own, orders, chunk, segments, last) in enumerate(jobs):
        copies += start_part(
            flat, core if own else 1 - core, orders, chunk, segments, last,
            refs[index], wides[index], grad_first, grad_second, sems[index],
        )
    for copy in copies:
        copy.wait()


def body(spatial_count, sample_count, volume, w_first, w_second, cotangent):
    count = spatial_count * sample_count
    bits = count.bit_length() - 1
    core_bit = spatial_count.bit_length() - 1
    others = [bit for bit in range(bits) if bit != core_bit]
    turn, rest = others[:3], others[3:]
    orders = [
        [tuple(turn[i] for i in turns) + tuple(rest) for turns in lane] for lane in LANE_TURNS
    ]
    steps = len(others) - 1
    lanes = len(LANE_TURNS)
    unit = 16 << steps
    second_rest = (27 - SPLIT) * LANES // 2
    segments = [
        [(0, SPLIT * LANES // 2, True, 0)],
        [(0, second_rest, True, SPLIT * LANES), (second_rest, FIRST // 2, False, 0)],
    ]
    chunks = [-(-2 * sum(seg[1] for seg in lane) // unit) * 16 for lane in segments]

    def swap_core(array):
        return lax.ppermute(array, BOTH, [(i, i ^ (1 << core_bit)) for i in range(count)])

    def swap(array, lane, step):
        pairs = []
        for i in range(count):
            bit = orders[lane][i.bit_count() % 2][step]
            pairs.append((i, i ^ (1 << bit) ^ (1 << core_bit)))
        return lax.ppermute(array, BOTH, pairs)

    slab = volume[0]
    depth = slab.shape[0]
    out_planes = depth // 4
    up = 2 * out_planes - 1
    slab_cot = cotangent[0]
    outside = pl.BlockSpec(memory_space=pl.ANY)
    far = pltpu.HBM
    face = slab[-3:]
    halo = lax.ppermute(
        face, "spatial", [(i, (i + 1) % spatial_count) for i in range(spatial_count)]
    )
    w2 = w_second
    x1_mid, x1_up, w1p = call(
        load_kernel,
        [
            ((64, 9 * 256), bf16),
            ((up * 64, 9 * 256), bf16),
            ((9 * 256, 128), bf16),
        ],
        pltpu.with_memory_space_constraint(slab, far),
        pltpu.with_memory_space_constraint(w_first, far),
        specs=[outside] * 2,
        scratch=[
            pltpu.VMEM(slab.shape, bf16),
            pltpu.VMEM(w_first.shape, bf16),
            pltpu.VMEM((depth - 1, 8, 24, LANES), f32),
            pltpu.SemaphoreType.DMA((3,)),
        ],
        after=(face,),
        cost=STEP_COST,
    )
    cells = out_planes * 16
    slope_up, picked_up, cot = call(
        upper_kernel,
        [
            ((up * 64, LANES), f32),
            ((up * 144, LANES), bf16),
            ((cells, 256), f32),
        ],
        x1_up,
        w1p,
        pltpu.with_memory_space_constraint(slab_cot, far),
        specs=[full(None), full(None), outside],
        scratch=[pltpu.VMEM(slab_cot.shape, bf16), pltpu.SemaphoreType.DMA((2,))],
        cost=pl.CostEstimate(flops=4 * 10**8, bytes_accessed=10**7, transcendentals=0),
    )
    rows = [chunk << steps for chunk in chunks]
    keep0, send0, x1_low, slope_low, x2, d2, own_first = call(
        functools.partial(lower_kernel, bits, spatial_count),
        [
            ((rows[0], LANES), f32),
            ((rows[0], LANES), bf16),
            ((128, 9 * 256), bf16),
            ((128, LANES), f32),
            ((cells, 27 * LANES), bf16),
            ((cells, 256), bf16),
            ((cells, 256), bf16),
        ],
        halo,
        x1_mid,
        w1p,
        picked_up,
        w2,
        cot,
        scratch=[pltpu.VMEM((3, 8, 24, LANES), f32), pltpu.VMEM((288, LANES), bf16)],
    )
    recv0 = swap_core(send0)
    keep1, send1 = call(
        functools.partial(last_kernel, bits, spatial_count),
        [((rows[1], LANES), f32), ((rows[1], LANES), bf16)],
        x1_up,
        x1_low,
        slope_up,
        slope_low,
        x2,
        d2,
        own_first,
        w2,
        scratch=[pltpu.VMEM((2 * FIRST, LANES), f32)],
        cost=pl.CostEstimate(flops=10**9, bytes_accessed=10**7, transcendentals=0),
    )
    recv1 = swap_core(send1)
    keep, recv = [keep0, keep1], [recv0, recv1]
    last = send1
    for step in range(steps):
        for lane in range(lanes):
            half = keep[lane].shape[0] // 2
            keep[lane], last = call(
                functools.partial(reduce_kernel, orders[lane], bits, step, spatial_count),
                [((half, LANES), f32), ((half, LANES), bf16)],
                keep[lane],
                recv[lane],
                after=(last,),
                cost=STEP_COST,
            )
            recv[lane] = swap(last, lane, step)
    for turn in range(2):
        for lane in range(lanes):
            shape = [((chunks[lane], LANES), bf16)]
            last = call(sum_kernel, shape, keep[lane], recv[lane], after=(last,), cost=STEP_COST)[0]
            keep[lane], recv[lane] = last, swap(last, lane, steps - turn)
    for step in reversed(range(1, steps)):
        for lane in range(lanes):
            shape = [((2 * keep[lane].shape[0], LANES), bf16)]
            last = call(
                join_kernel, shape, keep[lane], recv[lane], after=(last,), cost=STEP_COST
            )[0]
            keep[lane], recv[lane] = last, swap(last, lane, step - 1)
    held = [[keep[lane], None, swap_core(keep[lane]), None] for lane in range(lanes)]
    shapes = [jax.ShapeDtypeStruct((2 * FIRST, LANES), f32)]
    shapes += [jax.ShapeDtypeStruct((SECOND, 2 * LANES), f32)]
    token_shape = [jax.ShapeDtypeStruct((8, LANES), f32)]
    grads = []

    def write(group, grads, token):
        parts = [held[lane][which] for lane, which in group]
        jobs = [
            (which < 2, orders[lane], chunks[lane], segments[lane], which % 2 == 1)
            for lane, which in group
        ]
        return pl.pallas_call(
            functools.partial(final_kernel, bits, spatial_count, jobs, bool(grads)),
            out_shape=shapes + token_shape * token,
            in_specs=[full(part.shape) for part in parts] + [outside] * len(grads),
            out_specs=[outside] * 2 + [full(None)] * token,
            scratch_shapes=[pltpu.VMEM((rows[lane] // 2, LANES), f32) for lane, _ in group]
            + [pltpu.SemaphoreType.DMA(((1 << steps) + 1,)) for _ in group],
            input_output_aliases={len(parts): 0, len(parts) + 1: 1} if grads else {},
            compiler_params=params(),
            cost_estimate=STEP_COST,
        )(*parts, *grads)

    for lane, group in enumerate(WRITES[:lanes]):
        *grads, token = write(group, grads, 1)
        shape = [(recv[lane].shape, bf16)]
        last = call(copy_kernel, shape, recv[lane], after=(last, token), cost=STEP_COST)[0]
        held[lane][1], held[lane][3] = last, swap_core(last)
    for group in WRITES[lanes:]:
        grads = write(group, grads, 0)
    return grads


def solution(mesh):
    sizes = dict(mesh.shape)

    def run(*args):
        return tuple(body(sizes["spatial"], sizes["sample"], *args))

    return jax.shard_map(
        run,
        mesh=mesh,
        in_specs=(P("sample", "spatial", None, None), P(), P(), P("sample", "spatial", None, None)),
        out_specs=(P(), P()),
        check_vma=False,
    )
```

```python
import functools

import jax
import jax.numpy as jnp
from jax import lax
from jax.experimental import pallas as pl
from jax.experimental.pallas import tpu as pltpu
from jax.sharding import PartitionSpec as P

BOTH = ("sample", "spatial")
LANES = 128
SECOND, FIRST = 3456, 864
VMEM_BYTES = 32 * 1024 * 1024
SPLIT = 17
LANE_TURNS = (((0, 1, 2), (1, 2, 0)), ((2, 0, 1), (1, 2, 0)))
f32, bf16 = jnp.float32, jnp.bfloat16

WRITES = (((0, 0), (1, 0)), ((0, 2), (1, 2), (0, 1)), ((0, 3), (1, 1)), ((1, 3),))
STEP_COST = pl.CostEstimate(flops=4 * 10**9, bytes_accessed=8 * 10**7, transcendentals=0)


def full(shape):
    return pl.BlockSpec(memory_space=pltpu.VMEM)


def params():
    return pltpu.CompilerParams(vmem_limit_bytes=VMEM_BYTES)


def call(kernel, outs, *args, specs=None, scratch=(), cost=None, after=()):
    shapes = [jax.ShapeDtypeStruct(s, d) for s, d in outs]
    count = len(args)

    def run(*refs):
        kernel(*refs[:count], *refs[count + len(after) :])

    return pl.pallas_call(
        run,
        out_shape=shapes,
        in_specs=(specs or [full(a.shape) for a in args])
        + [pl.BlockSpec(memory_space=pl.ANY)] * len(after),
        out_specs=[full(s.shape) for s in shapes],
        scratch_shapes=scratch,
        compiler_params=params(),
        cost_estimate=cost,
    )(*args, *after)


def flat_index(spatial_count):
    return lax.axis_index("sample") * spatial_count + lax.axis_index("spatial")


def bit_of(value, bit):
    return lax.rem(lax.div(value, jnp.int32(1 << bit)), jnp.int32(2))


def half_of(flat, bits):
    total = jnp.int32(0)
    for bit in range(bits):
        total = total + bit_of(flat, bit)
    return lax.rem(total, jnp.int32(2))


def sigmoid(value):
    return 1.0 / (1.0 + jnp.exp(-value))


def slope_of(value, sig):
    return sig * (1.0 + value * (1.0 - sig))


def dot(a, b, dims=((1,), (0,))):
    return lax.dot_general(a, b, (dims, ((), ())), preferred_element_type=f32)


def selection():
    row = lax.broadcasted_iota(jnp.int32, (144, 64), 0)
    col = lax.broadcasted_iota(jnp.int32, (144, 64), 1)
    pair, cell = lax.div(row, 16), lax.rem(row, 16)
    b, c = lax.div(pair, 3), lax.rem(pair, 3)
    k, j = lax.div(cell, 4), lax.rem(cell, 4)
    x, y = lax.div(col, 8), lax.rem(col, 8)
    hit = (x == 2 * k + c - 1) & (y == 2 * j + b - 1)
    return hit.astype(f32).astype(bf16)


def fill(vpad, x1, planes, first_hidden, count):
    for index, (e, plane) in enumerate(planes):
        vpad[index, :, 0:8, :] = jnp.zeros((8, 8, LANES), f32)
        for kt in range(8):
            vpad[index, kt, 8:24, :] = plane[:, kt * LANES : (kt + 1) * LANES].astype(f32)
    for index, (e, plane) in enumerate(planes):
        for b in range(3):
            tiles = [jnp.zeros((8, LANES), f32)]
            for kt in range(8):
                tiles.append(vpad[index, kt, pl.ds(7 + b, 8, stride=2), :])
            for kk in range(4):
                left = jnp.concatenate([tiles[2 * kk], tiles[2 * kk + 1]], 0).astype(bf16)
                right = jnp.concatenate([tiles[2 * kk + 1], tiles[2 * kk + 2]], 0).astype(bf16)
                for a in range(e % 2, 3, 2):
                    h = (e - a) // 2 - first_hidden
                    if 0 <= h < count:
                        rows = slice(h * 64 + kk * 16, h * 64 + kk * 16 + 16)
                        col = (a * 3 + b) * 256
                        x1[rows, col : col + LANES] = left
                        x1[rows, col + LANES : col + 2 * LANES] = right


def load_kernel(vol_hbm, w1_hbm, x1_mid, x1, w1p, vol, w1, vpad, sems):
    loads = [
        pltpu.make_async_copy(vol_hbm, vol, sems.at[0]),
        pltpu.make_async_copy(w1_hbm, w1, sems.at[1]),
    ]
    for load in loads:
        load.start()
    loads[0].wait()
    depth = vol.shape[0]
    fill(vpad, x1_mid, [(e, vol[e - 3]) for e in (3, 4)], 1, 1)
    planes = [(e, vol[e - 3]) for e in range(4, depth + 3)]
    fill(vpad, x1, planes, 2, x1.shape[0] // 64)
    loads[1].wait()
    for ab in range(9):
        w1p[ab * 256 : ab * 256 + 64, :] = jnp.zeros((64, 128), bf16)
        w1p[ab * 256 + 64 : (ab + 1) * 256, :] = w1[ab * 192 : (ab + 1) * 192, :]


def hidden_of(x1, w1p, slope, picked):
    first_pre = dot(x1[...], w1p[...])
    sig = sigmoid(first_pre)
    hidden = (first_pre * sig).astype(bf16)
    slope[...] = slope_of(first_pre, sig)
    select = selection()
    planes = hidden.shape[0] // 64
    for h in range(0, planes, 2):
        pair = [hidden[g * 64 : (g + 1) * 64] for g in range(h, min(h + 2, planes))]
        cells = dot(select, jnp.concatenate(pair, 1)).astype(bf16)
        for g in range(len(pair)):
            at = (h + g) * 144
            picked[at : at + 144, :] = cells[:, g * LANES : (g + 1) * LANES]


def upper_kernel(x1, w1p, cot_hbm, slope, picked, cot, cot_in, sems):
    loads = [
        pltpu.make_async_copy(cot_hbm, cot_in, sems.at[0]),
    ]
    for load in loads:
        load.start()
    hidden_of(x1, w1p, slope, picked)
    loads[0].wait()
    row = lax.broadcasted_iota(jnp.int32, (16, 4), 0)
    col = lax.broadcasted_iota(jnp.int32, (16, 4), 1)
    for o in range(cot_in.shape[0]):
        cells = None
        for k in range(4):
            place = (row == 4 * k + col).astype(f32).astype(bf16)
            part = dot(place, cot_in[o, :, k * 256 : (k + 1) * 256])
            cells = part if cells is None else cells + part
        cot[o * 16 : (o + 1) * 16, :] = cells


def second_taps(x2, own_first, keep, send, first_tap, last_tap):
    columns = slice(first_tap * LANES, last_tap * LANES)
    rows = (last_tap - first_tap) * LANES // 2
    half = keep.shape[0] // 2
    grad = dot(x2[:, columns], own_first, ((0,), (0,)))
    for v in range(2):
        keep[v * half : v * half + rows, :] = grad[v * rows : (v + 1) * rows, :LANES]
        send[v * half : v * half + rows, :] = grad[v * rows : (v + 1) * rows, LANES:].astype(bf16)


def clear(keep, send, start):
    half = keep.shape[0] // 2
    if start < half:
        for v in range(2):
            rows = slice(v * half + start, (v + 1) * half)
            keep[rows, :] = jnp.zeros((half - start, LANES), f32)
            send[rows, :] = jnp.zeros((half - start, LANES), bf16)


def lower_kernel(
    bits, spatial_count, halo, x1_mid, w1p, picked_up, w2, cot,
    keep, send, x1, slope, x2, d2, own_first, vpad, picked,
):
    inside = jnp.where(lax.axis_index("spatial") > 0, 1.0, 0.0).astype(f32)
    planes = [(e, halo[e].astype(f32) * inside) for e in range(3)]
    fill(vpad, x1, planes, 0, 2)
    x1[64:128, 768:] = x1_mid[:, 768:]
    hidden_of(x1, w1p, slope, picked)
    out_planes = x2.shape[0] // 16
    for o in range(out_planes):
        for tap in range(27):
            h, pair = 2 * o + tap // 9, tap % 9
            if h < 2:
                cells = picked[h * 144 + pair * 16 : h * 144 + (pair + 1) * 16, :]
            else:
                at = (h - 2) * 144 + pair * 16
                cells = picked_up[at : at + 16, :]
            x2[o * 16 : (o + 1) * 16, tap * LANES : (tap + 1) * LANES] = cells
    second_pre = dot(x2[...], w2[...])
    sig = sigmoid(second_pre)
    delta = cot[...] * slope_of(second_pre, sig)
    d2[...] = delta.astype(bf16)
    core = half_of(flat_index(spatial_count), bits)
    left, right = delta[:, :LANES], delta[:, LANES:]
    own_first[...] = jnp.concatenate(
        [jnp.where(core == 0, left, right), jnp.where(core == 0, right, left)], 1
    ).astype(bf16)
    second_taps(x2, own_first[...], keep, send, 0, SPLIT)
    clear(keep, send, SPLIT * LANES // 2)


def last_kernel(
    bits, spatial_count, x1_up, x1_low, slope_up, slope_low, x2, d2, own_first, w2,
    keep, send, g1,
):
    second_taps(x2, own_first[...], keep, send, SPLIT, 27)
    out_planes = x2.shape[0] // 16
    hidden_planes = 2 * out_planes + 1
    select = selection()
    spread = dot(d2[...], w2[...], ((1,), (1,)))
    coarse = spread.astype(bf16)
    fine = (spread - coarse.astype(f32)).astype(bf16)
    deltas = []
    for h in range(hidden_planes):
        total = None
        for a in range(h % 2, 3, 2):
            o = (h - a) // 2
            if 0 <= o < out_planes:
                rows = slice(o * 16, (o + 1) * 16)
                stack = []
                for tap in range(a * 9, a * 9 + 9):
                    columns = slice(tap * LANES, (tap + 1) * LANES)
                    stack.append(jnp.concatenate([coarse[rows, columns], fine[rows, columns]], 1))
                both = dot(select, jnp.concatenate(stack, 0), ((0,), (0,)))
                part = both[:, :LANES] + both[:, LANES:]
                total = part if total is None else total + part
        rounded = total.astype(bf16).astype(f32)
        if h < 2:
            slope = slope_low[h * 64 : (h + 1) * 64]
        else:
            slope = slope_up[(h - 2) * 64 : (h - 1) * 64]
        deltas.append((rounded * slope).astype(bf16))
    d1_low, d1_up = jnp.concatenate(deltas[:2], 0), jnp.concatenate(deltas[2:], 0)
    for a in range(3):
        columns = slice(a * 768, (a + 1) * 768)
        grad = dot(d1_up, x1_up[:, columns], ((0,), (0,)))
        grad = (grad + dot(d1_low, x1_low[:, columns], ((0,), (0,)))).T
        for b in range(3):
            at = (a * 3 + b) * 192
            g1[at : at + 192, :] = grad[b * 256 + 64 : (b + 1) * 256]
    core = half_of(flat_index(spatial_count), bits)
    start, quarter = (27 - SPLIT) * LANES // 2, FIRST // 2
    for v in range(2):
        rows = slice(v * (keep.shape[0] // 2) + start, v * (keep.shape[0] // 2) + start + quarter)
        mine = pl.ds(pl.multiple_of(core * FIRST + v * quarter, 8), quarter)
        other = pl.ds(pl.multiple_of((1 - core) * FIRST + v * quarter, 8), quarter)
        keep[rows, :] = g1[mine, :]
        send[rows, :] = g1[other, :].astype(bf16)
    clear(keep, send, start + quarter)


def side_of(flat, orders, core, step):
    first, second = bit_of(flat, orders[0][step]), bit_of(flat, orders[1][step])
    return jnp.where(core == 0, first, second)


def reduce_kernel(orders, bits, step, spatial_count, keep, recv, kept, gone):
    half = keep.shape[0] // 2
    flat = flat_index(spatial_count)
    bit = side_of(flat, orders, half_of(flat, bits), step)
    mine = pl.ds(pl.multiple_of(bit * half, 16), half)
    other = pl.ds(pl.multiple_of((1 - bit) * half, 16), half)
    kept[...] = keep[mine, :] + recv[mine, :].astype(f32)
    gone[...] = (keep[other, :] + recv[other, :].astype(f32)).astype(bf16)


def sum_kernel(keep, recv, out):
    out[...] = (keep[...].astype(f32) + recv[...].astype(f32)).astype(bf16)


def join_kernel(own, recv, out):
    half = own.shape[0]
    out[0:half, :] = own[...]
    out[half:, :] = recv[...]


def copy_kernel(got, out):
    out[...] = got[...]


def start_part(flat, side, orders, chunk, segments, last, part, wide, grad_first, grad_second, sems):
    steps = len(orders[0]) - 1
    bits = [side_of(flat, orders, side, s) for s in range(steps)]
    columns = pl.ds(pl.multiple_of(side * LANES, LANES), LANES)
    top = 1 - bits[0] if last else bits[0]
    copies = []
    for place in range(1 << (steps - 1)):
        position = jnp.int32(0)
        for s in range(1, steps):
            want = (place >> (steps - 1 - s)) & 1
            differs = (1 - bits[s]) if want else bits[s]
            position = position + differs * (1 << (steps - 1 - s))
        at = place * chunk
        rows = pl.ds(pl.multiple_of(position * chunk, 16), chunk)
        wide[at : at + chunk, :] = part[rows, :].astype(f32)
        for start, size, second, base in segments:
            low, high = max(start, at), min(start + size, at + chunk)
            if low >= high:
                continue
            to = top * size + base + low - start
            if second:
                target = grad_second.at[pl.ds(pl.multiple_of(to, 16), high - low), columns]
            else:
                to = pl.multiple_of(side * FIRST + to, 16)
                target = grad_first.at[pl.ds(to, high - low)]
            copy = pltpu.make_async_copy(wide.at[low:high], target, sems.at[len(copies)])
            copy.start()
            copies.append(copy)
    return copies


def final_kernel(bits, spatial_count, jobs, chained, *refs):
    count = len(jobs)
    tokens = refs[count + 2 * chained + 2 : -2 * count]
    grad_first, grad_second = refs[count + 2 * chained : count + 2 * chained + 2]
    wides, sems = refs[-2 * count : -count], refs[-count:]
    flat = flat_index(spatial_count)
    core = half_of(flat, bits)
    for token in tokens:
        token[...] = jnp.zeros(token.shape, f32)
    copies = []
    for index, (own, orders, chunk, segments, last) in enumerate(jobs):
        copies += start_part(
            flat, core if own else 1 - core, orders, chunk, segments, last,
            refs[index], wides[index], grad_first, grad_second, sems[index],
        )
    for copy in copies:
        copy.wait()


def body(spatial_count, sample_count, volume, w_first, w_second, cotangent):
    count = spatial_count * sample_count
    bits = count.bit_length() - 1
    core_bit = spatial_count.bit_length() - 1
    others = [bit for bit in range(bits) if bit != core_bit]
    turn, rest = others[:3], others[3:]
    orders = [
        [tuple(turn[i] for i in turns) + tuple(rest) for turns in lane] for lane in LANE_TURNS
    ]
    steps = len(others) - 1
    lanes = len(LANE_TURNS)
    unit = 16 << steps
    second_rest = (27 - SPLIT) * LANES // 2
    segments = [
        [(0, SPLIT * LANES // 2, True, 0)],
        [(0, second_rest, True, SPLIT * LANES), (second_rest, FIRST // 2, False, 0)],
    ]
    chunks = [-(-2 * sum(seg[1] for seg in lane) // unit) * 16 for lane in segments]

    def swap_core(array):
        return lax.ppermute(array, BOTH, [(i, i ^ (1 << core_bit)) for i in range(count)])

    def swap(array, lane, step):
        pairs = []
        for i in range(count):
            bit = orders[lane][i.bit_count() % 2][step]
            pairs.append((i, i ^ (1 << bit) ^ (1 << core_bit)))
        return lax.ppermute(array, BOTH, pairs)

    slab = volume[0]
    depth = slab.shape[0]
    out_planes = depth // 4
    up = 2 * out_planes - 1
    slab_cot = cotangent[0]
    outside = pl.BlockSpec(memory_space=pl.ANY)
    far = pltpu.HBM
    face = slab[-3:]
    halo = lax.ppermute(
        face, "spatial", [(i, (i + 1) % spatial_count) for i in range(spatial_count)]
    )
    w2 = w_second
    x1_mid, x1_up, w1p = call(
        load_kernel,
        [
            ((64, 9 * 256), bf16),
            ((up * 64, 9 * 256), bf16),
            ((9 * 256, 128), bf16),
        ],
        pltpu.with_memory_space_constraint(slab, far),
        pltpu.with_memory_space_constraint(w_first, far),
        specs=[outside] * 2,
        scratch=[
            pltpu.VMEM(slab.shape, bf16),
            pltpu.VMEM(w_first.shape, bf16),
            pltpu.VMEM((depth - 1, 8, 24, LANES), f32),
            pltpu.SemaphoreType.DMA((3,)),
        ],
        after=(face,),
        cost=STEP_COST,
    )
    cells = out_planes * 16
    slope_up, picked_up, cot = call(
        upper_kernel,
        [
            ((up * 64, LANES), f32),
            ((up * 144, LANES), bf16),
            ((cells, 256), f32),
        ],
        x1_up,
        w1p,
        pltpu.with_memory_space_constraint(slab_cot, far),
        specs=[full(None), full(None), outside],
        scratch=[pltpu.VMEM(slab_cot.shape, bf16), pltpu.SemaphoreType.DMA((2,))],
        cost=pl.CostEstimate(flops=4 * 10**8, bytes_accessed=10**7, transcendentals=0),
    )
    rows = [chunk << steps for chunk in chunks]
    keep0, send0, x1_low, slope_low, x2, d2, own_first = call(
        functools.partial(lower_kernel, bits, spatial_count),
        [
            ((rows[0], LANES), f32),
            ((rows[0], LANES), bf16),
            ((128, 9 * 256), bf16),
            ((128, LANES), f32),
            ((cells, 27 * LANES), bf16),
            ((cells, 256), bf16),
            ((cells, 256), bf16),
        ],
        halo,
        x1_mid,
        w1p,
        picked_up,
        w2,
        cot,
        scratch=[pltpu.VMEM((3, 8, 24, LANES), f32), pltpu.VMEM((288, LANES), bf16)],
    )
    recv0 = swap_core(send0)
    keep1, send1 = call(
        functools.partial(last_kernel, bits, spatial_count),
        [((rows[1], LANES), f32), ((rows[1], LANES), bf16)],
        x1_up,
        x1_low,
        slope_up,
        slope_low,
        x2,
        d2,
        own_first,
        w2,
        scratch=[pltpu.VMEM((2 * FIRST, LANES), f32)],
        cost=pl.CostEstimate(flops=10**9, bytes_accessed=10**7, transcendentals=0),
    )
    recv1 = swap_core(send1)
    keep, recv = [keep0, keep1], [recv0, recv1]
    last = send1
    for step in range(steps):
        for lane in range(lanes):
            half = keep[lane].shape[0] // 2
            keep[lane], last = call(
                functools.partial(reduce_kernel, orders[lane], bits, step, spatial_count),
                [((half, LANES), f32), ((half, LANES), bf16)],
                keep[lane],
                recv[lane],
                after=(last,),
                cost=STEP_COST,
            )
            recv[lane] = swap(last, lane, step)
    for turn in range(2):
        for lane in range(lanes):
            shape = [((chunks[lane], LANES), bf16)]
            last = call(sum_kernel, shape, keep[lane], recv[lane], after=(last,), cost=STEP_COST)[0]
            keep[lane], recv[lane] = last, swap(last, lane, steps - turn)
    for step in reversed(range(1, steps)):
        for lane in range(lanes):
            shape = [((2 * keep[lane].shape[0], LANES), bf16)]
            last = call(
                join_kernel, shape, keep[lane], recv[lane], after=(last,), cost=STEP_COST
            )[0]
            keep[lane], recv[lane] = last, swap(last, lane, step - 1)
    held = [[keep[lane], None, None, None] for lane in range(lanes)]
    shapes = [jax.ShapeDtypeStruct((2 * FIRST, LANES), f32)]
    shapes += [jax.ShapeDtypeStruct((SECOND, 2 * LANES), f32)]
    token_shape = [jax.ShapeDtypeStruct((8, LANES), f32)]
    grads = []

    def write(group, grads, token):
        parts = [held[lane][which] for lane, which in group]
        jobs = [
            (which < 2, orders[lane], chunks[lane], segments[lane], which % 2 == 1)
            for lane, which in group
        ]
        return pl.pallas_call(
            functools.partial(final_kernel, bits, spatial_count, jobs, bool(grads)),
            out_shape=shapes + token_shape * token,
            in_specs=[full(part.shape) for part in parts] + [outside] * len(grads),
            out_specs=[outside] * 2 + [full(None)] * token,
            scratch_shapes=[pltpu.VMEM((rows[lane] // 2, LANES), f32) for lane, _ in group]
            + [pltpu.SemaphoreType.DMA(((1 << steps) + 1,)) for _ in group],
            input_output_aliases={len(parts): 0, len(parts) + 1: 1} if grads else {},
            compiler_params=params(),
            cost_estimate=STEP_COST,
        )(*parts, *grads)

    def copied(array, after):
        return call(copy_kernel, [(array.shape, bf16)], array, after=after, cost=STEP_COST)[0]

    for lane, group in enumerate(WRITES[:lanes]):
        *grads, token = write(group, grads, 1)
        if lane == 0:
            for part in held:
                part[2] = swap_core(copied(part[0], (token,)))
        last = copied(recv[lane], (last, token))
        held[lane][1], held[lane][3] = last, swap_core(last)
    for group in WRITES[lanes:]:
        grads = write(group, grads, 0)
    return grads


def solution(mesh):
    sizes = dict(mesh.shape)

    def run(*args):
        return tuple(body(sizes["spatial"], sizes["sample"], *args))

    return jax.shard_map(
        run,
        mesh=mesh,
        in_specs=(P("sample", "spatial", None, None), P(), P(), P("sample", "spatial", None, None)),
        out_specs=(P(), P()),
        check_vma=False,
    )
```

```python
import functools

import jax
import jax.numpy as jnp
from jax import lax
from jax.experimental import pallas as pl
from jax.experimental.pallas import tpu as pltpu
from jax.sharding import PartitionSpec as P

BOTH = ("sample", "spatial")
LANES = 128
SECOND, FIRST = 3456, 864
VMEM_BYTES = 32 * 1024 * 1024
SPLIT = 17
LANE_TURNS = (((0, 1, 2), (1, 2, 0)), ((2, 0, 1), (1, 2, 0)))
f32, bf16 = jnp.float32, jnp.bfloat16

WRITES = (((0, 0), (1, 0)), ((0, 2), (1, 2), (0, 1)), ((0, 3), (1, 1)), ((1, 3),))
STEP_COST = pl.CostEstimate(flops=4 * 10**9, bytes_accessed=8 * 10**7, transcendentals=0)


def full(shape):
    return pl.BlockSpec(memory_space=pltpu.VMEM)


def params():
    return pltpu.CompilerParams(vmem_limit_bytes=VMEM_BYTES)


def call(kernel, outs, *args, specs=None, scratch=(), cost=None, after=()):
    shapes = [jax.ShapeDtypeStruct(s, d) for s, d in outs]
    count = len(args)

    def run(*refs):
        kernel(*refs[:count], *refs[count + len(after) :])

    return pl.pallas_call(
        run,
        out_shape=shapes,
        in_specs=(specs or [full(a.shape) for a in args])
        + [pl.BlockSpec(memory_space=pl.ANY)] * len(after),
        out_specs=[full(s.shape) for s in shapes],
        scratch_shapes=scratch,
        compiler_params=params(),
        cost_estimate=cost,
    )(*args, *after)


def flat_index(spatial_count):
    return lax.axis_index("sample") * spatial_count + lax.axis_index("spatial")


def bit_of(value, bit):
    return lax.rem(lax.div(value, jnp.int32(1 << bit)), jnp.int32(2))


def half_of(flat, bits):
    total = jnp.int32(0)
    for bit in range(bits):
        total = total + bit_of(flat, bit)
    return lax.rem(total, jnp.int32(2))


def sigmoid(value):
    return 1.0 / (1.0 + jnp.exp(-value))


def slope_of(value, sig):
    return sig * (1.0 + value * (1.0 - sig))


def dot(a, b, dims=((1,), (0,))):
    return lax.dot_general(a, b, (dims, ((), ())), preferred_element_type=f32)


def selection():
    row = lax.broadcasted_iota(jnp.int32, (144, 64), 0)
    col = lax.broadcasted_iota(jnp.int32, (144, 64), 1)
    pair, cell = lax.div(row, 16), lax.rem(row, 16)
    b, c = lax.div(pair, 3), lax.rem(pair, 3)
    k, j = lax.div(cell, 4), lax.rem(cell, 4)
    x, y = lax.div(col, 8), lax.rem(col, 8)
    hit = (x == 2 * k + c - 1) & (y == 2 * j + b - 1)
    return hit.astype(f32).astype(bf16)


def fill(vpad, x1, planes, first_hidden, count):
    for index, (e, plane) in enumerate(planes):
        vpad[index, :, 0:8, :] = jnp.zeros((8, 8, LANES), f32)
        for kt in range(8):
            vpad[index, kt, 8:24, :] = plane[:, kt * LANES : (kt + 1) * LANES].astype(f32)
    for index, (e, plane) in enumerate(planes):
        for b in range(3):
            tiles = [jnp.zeros((8, LANES), f32)]
            for kt in range(8):
                tiles.append(vpad[index, kt, pl.ds(7 + b, 8, stride=2), :])
            for kk in range(4):
                left = jnp.concatenate([tiles[2 * kk], tiles[2 * kk + 1]], 0).astype(bf16)
                right = jnp.concatenate([tiles[2 * kk + 1], tiles[2 * kk + 2]], 0).astype(bf16)
                for a in range(e % 2, 3, 2):
                    h = (e - a) // 2 - first_hidden
                    if 0 <= h < count:
                        rows = slice(h * 64 + kk * 16, h * 64 + kk * 16 + 16)
                        col = (a * 3 + b) * 256
                        x1[rows, col : col + LANES] = left
                        x1[rows, col + LANES : col + 2 * LANES] = right


def load_kernel(vol_hbm, w1_hbm, x1_mid, x1, w1p, vol, w1, vpad, sems):
    loads = [
        pltpu.make_async_copy(vol_hbm, vol, sems.at[0]),
        pltpu.make_async_copy(w1_hbm, w1, sems.at[1]),
    ]
    for load in loads:
        load.start()
    loads[0].wait()
    depth = vol.shape[0]
    fill(vpad, x1_mid, [(e, vol[e - 3]) for e in (3, 4)], 1, 1)
    planes = [(e, vol[e - 3]) for e in range(4, depth + 3)]
    fill(vpad, x1, planes, 2, x1.shape[0] // 64)
    loads[1].wait()
    for ab in range(9):
        w1p[ab * 256 : ab * 256 + 64, :] = jnp.zeros((64, 128), bf16)
        w1p[ab * 256 + 64 : (ab + 1) * 256, :] = w1[ab * 192 : (ab + 1) * 192, :]


def hidden_of(x1, w1p, slope, picked):
    first_pre = dot(x1[...], w1p[...])
    sig = sigmoid(first_pre)
    hidden = (first_pre * sig).astype(bf16)
    slope[...] = slope_of(first_pre, sig)
    select = selection()
    planes = hidden.shape[0] // 64
    for h in range(0, planes, 2):
        pair = [hidden[g * 64 : (g + 1) * 64] for g in range(h, min(h + 2, planes))]
        cells = dot(select, jnp.concatenate(pair, 1)).astype(bf16)
        for g in range(len(pair)):
            at = (h + g) * 144
            picked[at : at + 144, :] = cells[:, g * LANES : (g + 1) * LANES]


def upper_kernel(x1, w1p, cot_hbm, slope, picked, cot, cot_in, sems):
    loads = [
        pltpu.make_async_copy(cot_hbm, cot_in, sems.at[0]),
    ]
    for load in loads:
        load.start()
    hidden_of(x1, w1p, slope, picked)
    loads[0].wait()
    row = lax.broadcasted_iota(jnp.int32, (16, 4), 0)
    col = lax.broadcasted_iota(jnp.int32, (16, 4), 1)
    for o in range(cot_in.shape[0]):
        cells = None
        for k in range(4):
            place = (row == 4 * k + col).astype(f32).astype(bf16)
            part = dot(place, cot_in[o, :, k * 256 : (k + 1) * 256])
            cells = part if cells is None else cells + part
        cot[o * 16 : (o + 1) * 16, :] = cells


def second_taps(x2, own_first, keep, send, first_tap, last_tap):
    columns = slice(first_tap * LANES, last_tap * LANES)
    rows = (last_tap - first_tap) * LANES // 2
    half = keep.shape[0] // 2
    grad = dot(x2[:, columns], own_first, ((0,), (0,)))
    for v in range(2):
        keep[v * half : v * half + rows, :] = grad[v * rows : (v + 1) * rows, :LANES]
        send[v * half : v * half + rows, :] = grad[v * rows : (v + 1) * rows, LANES:].astype(bf16)


def clear(keep, send, start):
    half = keep.shape[0] // 2
    if start < half:
        for v in range(2):
            rows = slice(v * half + start, (v + 1) * half)
            keep[rows, :] = jnp.zeros((half - start, LANES), f32)
            send[rows, :] = jnp.zeros((half - start, LANES), bf16)


def lower_kernel(
    bits, spatial_count, halo, x1_mid, w1p, picked_up, w2, cot,
    keep, send, x1, slope, x2, d2, own_first, vpad, picked,
):
    inside = jnp.where(lax.axis_index("spatial") > 0, 1.0, 0.0).astype(f32)
    planes = [(e, halo[e].astype(f32) * inside) for e in range(3)]
    fill(vpad, x1, planes, 0, 2)
    x1[64:128, 768:] = x1_mid[:, 768:]
    hidden_of(x1, w1p, slope, picked)
    out_planes = x2.shape[0] // 16
    for o in range(out_planes):
        for tap in range(27):
            h, pair = 2 * o + tap // 9, tap % 9
            if h < 2:
                cells = picked[h * 144 + pair * 16 : h * 144 + (pair + 1) * 16, :]
            else:
                at = (h - 2) * 144 + pair * 16
                cells = picked_up[at : at + 16, :]
            x2[o * 16 : (o + 1) * 16, tap * LANES : (tap + 1) * LANES] = cells
    second_pre = dot(x2[...], w2[...])
    sig = sigmoid(second_pre)
    delta = cot[...] * slope_of(second_pre, sig)
    d2[...] = delta.astype(bf16)
    core = half_of(flat_index(spatial_count), bits)
    left, right = delta[:, :LANES], delta[:, LANES:]
    own_first[...] = jnp.concatenate(
        [jnp.where(core == 0, left, right), jnp.where(core == 0, right, left)], 1
    ).astype(bf16)
    second_taps(x2, own_first[...], keep, send, 0, SPLIT)
    clear(keep, send, SPLIT * LANES // 2)


def last_kernel(
    bits, spatial_count, x1_up, x1_low, slope_up, slope_low, x2, d2, own_first, w2,
    keep, send, g1,
):
    second_taps(x2, own_first[...], keep, send, SPLIT, 27)
    out_planes = x2.shape[0] // 16
    hidden_planes = 2 * out_planes + 1
    select = selection()
    spread = dot(d2[...], w2[...], ((1,), (1,)))
    coarse = spread.astype(bf16)
    fine = (spread - coarse.astype(f32)).astype(bf16)
    deltas = []
    for h in range(hidden_planes):
        total = None
        for a in range(h % 2, 3, 2):
            o = (h - a) // 2
            if 0 <= o < out_planes:
                rows = slice(o * 16, (o + 1) * 16)
                stack = []
                for tap in range(a * 9, a * 9 + 9):
                    columns = slice(tap * LANES, (tap + 1) * LANES)
                    stack.append(jnp.concatenate([coarse[rows, columns], fine[rows, columns]], 1))
                both = dot(select, jnp.concatenate(stack, 0), ((0,), (0,)))
                part = both[:, :LANES] + both[:, LANES:]
                total = part if total is None else total + part
        rounded = total.astype(bf16).astype(f32)
        if h < 2:
            slope = slope_low[h * 64 : (h + 1) * 64]
        else:
            slope = slope_up[(h - 2) * 64 : (h - 1) * 64]
        deltas.append((rounded * slope).astype(bf16))
    d1_low, d1_up = jnp.concatenate(deltas[:2], 0), jnp.concatenate(deltas[2:], 0)
    for a in range(3):
        columns = slice(a * 768, (a + 1) * 768)
        grad = dot(d1_up, x1_up[:, columns], ((0,), (0,)))
        grad = (grad + dot(d1_low, x1_low[:, columns], ((0,), (0,)))).T
        for b in range(3):
            at = (a * 3 + b) * 192
            g1[at : at + 192, :] = grad[b * 256 + 64 : (b + 1) * 256]
    core = half_of(flat_index(spatial_count), bits)
    start, quarter = (27 - SPLIT) * LANES // 2, FIRST // 2
    for v in range(2):
        rows = slice(v * (keep.shape[0] // 2) + start, v * (keep.shape[0] // 2) + start + quarter)
        mine = pl.ds(pl.multiple_of(core * FIRST + v * quarter, 8), quarter)
        other = pl.ds(pl.multiple_of((1 - core) * FIRST + v * quarter, 8), quarter)
        keep[rows, :] = g1[mine, :]
        send[rows, :] = g1[other, :].astype(bf16)
    clear(keep, send, start + quarter)


def side_of(flat, orders, core, step):
    first, second = bit_of(flat, orders[0][step]), bit_of(flat, orders[1][step])
    return jnp.where(core == 0, first, second)


def reduce_kernel(orders, bits, step, spatial_count, keep, recv, kept, gone):
    half = keep.shape[0] // 2
    flat = flat_index(spatial_count)
    bit = side_of(flat, orders, half_of(flat, bits), step)
    mine = pl.ds(pl.multiple_of(bit * half, 16), half)
    other = pl.ds(pl.multiple_of((1 - bit) * half, 16), half)
    kept[...] = keep[mine, :] + recv[mine, :].astype(f32)
    gone[...] = (keep[other, :] + recv[other, :].astype(f32)).astype(bf16)


def sum_kernel(keep, recv, out):
    out[...] = (keep[...].astype(f32) + recv[...].astype(f32)).astype(bf16)


def join_kernel(own, recv, out):
    half = own.shape[0]
    out[0:half, :] = own[...]
    out[half:, :] = recv[...]


def copy_kernel(got, out):
    out[...] = got[...]


def start_part(flat, side, orders, chunk, segments, last, part, wide, grad_first, grad_second, sems):
    steps = len(orders[0]) - 1
    bits = [side_of(flat, orders, side, s) for s in range(steps)]
    columns = pl.ds(pl.multiple_of(side * LANES, LANES), LANES)
    top = 1 - bits[0] if last else bits[0]
    copies = []
    for place in range(1 << (steps - 1)):
        position = jnp.int32(0)
        for s in range(1, steps):
            want = (place >> (steps - 1 - s)) & 1
            differs = (1 - bits[s]) if want else bits[s]
            position = position + differs * (1 << (steps - 1 - s))
        at = place * chunk
        rows = pl.ds(pl.multiple_of(position * chunk, 16), chunk)
        wide[at : at + chunk, :] = part[rows, :].astype(f32)
        for start, size, second, base in segments:
            low, high = max(start, at), min(start + size, at + chunk)
            if low >= high:
                continue
            to = top * size + base + low - start
            if second:
                target = grad_second.at[pl.ds(pl.multiple_of(to, 16), high - low), columns]
            else:
                to = pl.multiple_of(side * FIRST + to, 16)
                target = grad_first.at[pl.ds(to, high - low)]
            copy = pltpu.make_async_copy(wide.at[low:high], target, sems.at[len(copies)])
            copy.start()
            copies.append(copy)
    return copies


def final_kernel(bits, spatial_count, jobs, chained, *refs):
    count = len(jobs)
    tokens = refs[count + 2 * chained + 2 : -2 * count]
    grad_first, grad_second = refs[count + 2 * chained : count + 2 * chained + 2]
    wides, sems = refs[-2 * count : -count], refs[-count:]
    flat = flat_index(spatial_count)
    core = half_of(flat, bits)
    for token in tokens:
        token[...] = jnp.zeros(token.shape, f32)
    copies = []
    for index, (own, orders, chunk, segments, last) in enumerate(jobs):
        copies += start_part(
            flat, core if own else 1 - core, orders, chunk, segments, last,
            refs[index], wides[index], grad_first, grad_second, sems[index],
        )
    for copy in copies:
        copy.wait()


def body(spatial_count, sample_count, volume, w_first, w_second, cotangent):
    count = spatial_count * sample_count
    bits = count.bit_length() - 1
    core_bit = spatial_count.bit_length() - 1
    others = [bit for bit in range(bits) if bit != core_bit]
    turn, rest = others[:3], others[3:]
    orders = [
        [tuple(turn[i] for i in turns) + tuple(rest) for turns in lane] for lane in LANE_TURNS
    ]
    steps = len(others) - 1
    lanes = len(LANE_TURNS)
    unit = 16 << steps
    second_rest = (27 - SPLIT) * LANES // 2
    segments = [
        [(0, SPLIT * LANES // 2, True, 0)],
        [(0, second_rest, True, SPLIT * LANES), (second_rest, FIRST // 2, False, 0)],
    ]
    chunks = [-(-2 * sum(seg[1] for seg in lane) // unit) * 16 for lane in segments]

    def swap_core(array):
        return lax.ppermute(array, BOTH, [(i, i ^ (1 << core_bit)) for i in range(count)])

    def swap(array, lane, step):
        pairs = []
        for i in range(count):
            bit = orders[lane][i.bit_count() % 2][step]
            pairs.append((i, i ^ (1 << bit) ^ (1 << core_bit)))
        return lax.ppermute(array, BOTH, pairs)

    slab = volume[0]
    depth = slab.shape[0]
    out_planes = depth // 4
    up = 2 * out_planes - 1
    slab_cot = cotangent[0]
    outside = pl.BlockSpec(memory_space=pl.ANY)
    far = pltpu.HBM
    face = slab[-3:]
    halo = lax.ppermute(
        face, "spatial", [(i, (i + 1) % spatial_count) for i in range(spatial_count)]
    )
    w2 = w_second
    x1_mid, x1_up, w1p = call(
        load_kernel,
        [
            ((64, 9 * 256), bf16),
            ((up * 64, 9 * 256), bf16),
            ((9 * 256, 128), bf16),
        ],
        pltpu.with_memory_space_constraint(slab, far),
        pltpu.with_memory_space_constraint(w_first, far),
        specs=[outside] * 2,
        scratch=[
            pltpu.VMEM(slab.shape, bf16),
            pltpu.VMEM(w_first.shape, bf16),
            pltpu.VMEM((depth - 1, 8, 32, LANES), f32),
            pltpu.SemaphoreType.DMA((3,)),
        ],
        after=(face,),
        cost=STEP_COST,
    )
    cells = out_planes * 16
    slope_up, picked_up, cot = call(
        upper_kernel,
        [
            ((up * 64, LANES), f32),
            ((up * 144, LANES), bf16),
            ((cells, 256), f32),
        ],
        x1_up,
        w1p,
        pltpu.with_memory_space_constraint(slab_cot, far),
        specs=[full(None), full(None), outside],
        scratch=[pltpu.VMEM(slab_cot.shape, bf16), pltpu.SemaphoreType.DMA((2,))],
        cost=pl.CostEstimate(flops=4 * 10**8, bytes_accessed=10**7, transcendentals=0),
    )
    rows = [chunk << steps for chunk in chunks]
    keep0, send0, x1_low, slope_low, x2, d2, own_first = call(
        functools.partial(lower_kernel, bits, spatial_count),
        [
            ((rows[0], LANES), f32),
            ((rows[0], LANES), bf16),
            ((128, 9 * 256), bf16),
            ((128, LANES), f32),
            ((cells, 27 * LANES), bf16),
            ((cells, 256), bf16),
            ((cells, 256), bf16),
        ],
        halo,
        x1_mid,
        w1p,
        picked_up,
        w2,
        cot,
        scratch=[pltpu.VMEM((3, 8, 32, LANES), f32), pltpu.VMEM((288, LANES), bf16)],
    )
    recv0 = swap_core(send0)
    keep1, send1 = call(
        functools.partial(last_kernel, bits, spatial_count),
        [((rows[1], LANES), f32), ((rows[1], LANES), bf16)],
        x1_up,
        x1_low,
        slope_up,
        slope_low,
        x2,
        d2,
        own_first,
        w2,
        scratch=[pltpu.VMEM((2 * FIRST, LANES), f32)],
        cost=pl.CostEstimate(flops=10**9, bytes_accessed=10**7, transcendentals=0),
    )
    recv1 = swap_core(send1)
    keep, recv = [keep0, keep1], [recv0, recv1]
    last = send1
    for step in range(steps):
        for lane in range(lanes):
            half = keep[lane].shape[0] // 2
            keep[lane], last = call(
                functools.partial(reduce_kernel, orders[lane], bits, step, spatial_count),
                [((half, LANES), f32), ((half, LANES), bf16)],
                keep[lane],
                recv[lane],
                after=(last,),
                cost=STEP_COST,
            )
            recv[lane] = swap(last, lane, step)
    for turn in range(2):
        for lane in range(lanes):
            shape = [((chunks[lane], LANES), bf16)]
            last = call(sum_kernel, shape, keep[lane], recv[lane], after=(last,), cost=STEP_COST)[0]
            keep[lane], recv[lane] = last, swap(last, lane, steps - turn)
    for step in reversed(range(1, steps)):
        for lane in range(lanes):
            shape = [((2 * keep[lane].shape[0], LANES), bf16)]
            last = call(
                join_kernel, shape, keep[lane], recv[lane], after=(last,), cost=STEP_COST
            )[0]
            keep[lane], recv[lane] = last, swap(last, lane, step - 1)
    held = [[keep[lane], None, None, None] for lane in range(lanes)]
    shapes = [jax.ShapeDtypeStruct((2 * FIRST, LANES), f32)]
    shapes += [jax.ShapeDtypeStruct((SECOND, 2 * LANES), f32)]
    token_shape = [jax.ShapeDtypeStruct((8, LANES), f32)]
    grads = []

    def write(group, grads, token):
        parts = [held[lane][which] for lane, which in group]
        jobs = [
            (which < 2, orders[lane], chunks[lane], segments[lane], which % 2 == 1)
            for lane, which in group
        ]
        return pl.pallas_call(
            functools.partial(final_kernel, bits, spatial_count, jobs, bool(grads)),
            out_shape=shapes + token_shape * token,
            in_specs=[full(part.shape) for part in parts] + [outside] * len(grads),
            out_specs=[outside] * 2 + [full(None)] * token,
            scratch_shapes=[pltpu.VMEM((rows[lane] // 2, LANES), f32) for lane, _ in group]
            + [pltpu.SemaphoreType.DMA(((1 << steps) + 1,)) for _ in group],
            input_output_aliases={len(parts): 0, len(parts) + 1: 1} if grads else {},
            compiler_params=params(),
            cost_estimate=STEP_COST,
        )(*parts, *grads)

    def copied(array, after):
        return call(copy_kernel, [(array.shape, bf16)], array, after=after, cost=STEP_COST)[0]

    for lane, group in enumerate(WRITES[:lanes]):
        *grads, token = write(group, grads, 1)
        if lane == 0:
            for part in held:
                part[2] = swap_core(copied(part[0], (token,)))
        last = copied(recv[lane], (last, token))
        held[lane][1], held[lane][3] = last, swap_core(last)
    for group in WRITES[lanes:]:
        grads = write(group, grads, 0)
    return grads


def solution(mesh):
    sizes = dict(mesh.shape)

    def run(*args):
        return tuple(body(sizes["spatial"], sizes["sample"], *args))

    return jax.shard_map(
        run,
        mesh=mesh,
        in_specs=(P("sample", "spatial", None, None), P(), P(), P("sample", "spatial", None, None)),
        out_specs=(P(), P()),
        check_vma=False,
    )
```

```python
import functools

import jax
import jax.numpy as jnp
from jax import lax
from jax.experimental import pallas as pl
from jax.experimental.pallas import tpu as pltpu
from jax.sharding import PartitionSpec as P

BOTH = ("sample", "spatial")
LANES = 128
SECOND, FIRST = 3456, 864
VMEM_BYTES = 32 * 1024 * 1024
SPLIT = 17
LANE_TURNS = (((0, 1, 2), (1, 2, 0)), ((2, 0, 1), (1, 2, 0)))
f32, bf16 = jnp.float32, jnp.bfloat16

WRITES = (((0, 0), (1, 0)), ((0, 2), (1, 2), (0, 1)), ((0, 3), (1, 1)), ((1, 3),))
STEP_COST = pl.CostEstimate(flops=4 * 10**9, bytes_accessed=8 * 10**7, transcendentals=0)


def full(shape):
    return pl.BlockSpec(memory_space=pltpu.VMEM)


def params():
    return pltpu.CompilerParams(vmem_limit_bytes=VMEM_BYTES)


def call(kernel, outs, *args, specs=None, scratch=(), cost=None, after=()):
    shapes = [jax.ShapeDtypeStruct(s, d) for s, d in outs]
    count = len(args)

    def run(*refs):
        kernel(*refs[:count], *refs[count + len(after) :])

    return pl.pallas_call(
        run,
        out_shape=shapes,
        in_specs=(specs or [full(a.shape) for a in args])
        + [pl.BlockSpec(memory_space=pl.ANY)] * len(after),
        out_specs=[full(s.shape) for s in shapes],
        scratch_shapes=scratch,
        compiler_params=params(),
        cost_estimate=cost,
    )(*args, *after)


def flat_index(spatial_count):
    return lax.axis_index("sample") * spatial_count + lax.axis_index("spatial")


def bit_of(value, bit):
    return lax.rem(lax.div(value, jnp.int32(1 << bit)), jnp.int32(2))


def half_of(flat, bits):
    total = jnp.int32(0)
    for bit in range(bits):
        total = total + bit_of(flat, bit)
    return lax.rem(total, jnp.int32(2))


def sigmoid(value):
    return 1.0 / (1.0 + jnp.exp(-value))


def slope_of(value, sig):
    return sig * (1.0 + value * (1.0 - sig))


def dot(a, b, dims=((1,), (0,))):
    return lax.dot_general(a, b, (dims, ((), ())), preferred_element_type=f32)


def selection():
    row = lax.broadcasted_iota(jnp.int32, (144, 64), 0)
    col = lax.broadcasted_iota(jnp.int32, (144, 64), 1)
    pair, cell = lax.div(row, 16), lax.rem(row, 16)
    b, c = lax.div(pair, 3), lax.rem(pair, 3)
    k, j = lax.div(cell, 4), lax.rem(cell, 4)
    x, y = lax.div(col, 8), lax.rem(col, 8)
    hit = (x == 2 * k + c - 1) & (y == 2 * j + b - 1)
    return hit.astype(f32).astype(bf16)


def fill(vpad, x1, planes, first_hidden, count):
    for index, (e, plane) in enumerate(planes):
        vpad[index, :, 0:8, :] = jnp.zeros((8, 8, LANES), f32)
        for kt in range(8):
            vpad[index, kt, 8:24, :] = plane[:, kt * LANES : (kt + 1) * LANES].astype(f32)
    for index, (e, plane) in enumerate(planes):
        for b in range(3):
            tiles = [jnp.zeros((8, LANES), f32)]
            for kt in range(8):
                tiles.append(vpad[index, kt, pl.ds(7 + b, 8, stride=2), :])
            for kk in range(4):
                left = jnp.concatenate([tiles[2 * kk], tiles[2 * kk + 1]], 0).astype(bf16)
                right = jnp.concatenate([tiles[2 * kk + 1], tiles[2 * kk + 2]], 0).astype(bf16)
                for a in range(e % 2, 3, 2):
                    h = (e - a) // 2 - first_hidden
                    if 0 <= h < count:
                        rows = slice(h * 64 + kk * 16, h * 64 + kk * 16 + 16)
                        col = (a * 3 + b) * 256
                        x1[rows, col : col + LANES] = left
                        x1[rows, col + LANES : col + 2 * LANES] = right


def load_kernel(vol_hbm, w1_hbm, x1_mid, x1, w1p, vol, w1, vpad, sems):
    loads = [
        pltpu.make_async_copy(vol_hbm, vol, sems.at[0]),
        pltpu.make_async_copy(w1_hbm, w1, sems.at[1]),
    ]
    for load in loads:
        load.start()
    loads[0].wait()
    depth = vol.shape[0]
    fill(vpad, x1_mid, [(e, vol[e - 3]) for e in (3, 4)], 1, 1)
    planes = [(e, vol[e - 3]) for e in range(4, depth + 3)]
    fill(vpad, x1, planes, 2, x1.shape[0] // 64)
    loads[1].wait()
    for ab in range(9):
        w1p[ab * 256 : ab * 256 + 64, :] = jnp.zeros((64, 128), bf16)
        w1p[ab * 256 + 64 : (ab + 1) * 256, :] = w1[ab * 192 : (ab + 1) * 192, :]


def hidden_of(x1, w1p, slope, picked):
    first_pre = dot(x1[...], w1p[...])
    sig = sigmoid(first_pre)
    hidden = (first_pre * sig).astype(bf16)
    slope[...] = slope_of(first_pre, sig)
    select = selection()
    planes = hidden.shape[0] // 64
    for h in range(0, planes, 2):
        pair = [hidden[g * 64 : (g + 1) * 64] for g in range(h, min(h + 2, planes))]
        cells = dot(select, jnp.concatenate(pair, 1)).astype(bf16)
        for g in range(len(pair)):
            at = (h + g) * 144
            picked[at : at + 144, :] = cells[:, g * LANES : (g + 1) * LANES]


def upper_kernel(x1, w1p, cot_hbm, slope, picked, cot, cot_in, sems):
    loads = [
        pltpu.make_async_copy(cot_hbm, cot_in, sems.at[0]),
    ]
    for load in loads:
        load.start()
    hidden_of(x1, w1p, slope, picked)
    loads[0].wait()
    row = lax.broadcasted_iota(jnp.int32, (16, 4), 0)
    col = lax.broadcasted_iota(jnp.int32, (16, 4), 1)
    for o in range(cot_in.shape[0]):
        cells = None
        for k in range(4):
            place = (row == 4 * k + col).astype(f32).astype(bf16)
            part = dot(place, cot_in[o, :, k * 256 : (k + 1) * 256])
            cells = part if cells is None else cells + part
        cot[o * 16 : (o + 1) * 16, :] = cells


def second_taps(x2, own_first, keep, send, first_tap, last_tap):
    columns = slice(first_tap * LANES, last_tap * LANES)
    rows = (last_tap - first_tap) * LANES // 2
    half = keep.shape[0] // 2
    grad = dot(x2[:, columns], own_first, ((0,), (0,)))
    for v in range(2):
        keep[v * half : v * half + rows, :] = grad[v * rows : (v + 1) * rows, :LANES]
        send[v * half : v * half + rows, :] = grad[v * rows : (v + 1) * rows, LANES:].astype(bf16)


def clear(keep, send, start):
    half = keep.shape[0] // 2
    if start < half:
        for v in range(2):
            rows = slice(v * half + start, (v + 1) * half)
            keep[rows, :] = jnp.zeros((half - start, LANES), f32)
            send[rows, :] = jnp.zeros((half - start, LANES), bf16)


def lower_kernel(
    bits, spatial_count, halo, x1_mid, w1p, picked_up, w2, cot,
    keep, send, x1, slope, x2, d2, own_first, vpad, picked,
):
    inside = jnp.where(lax.axis_index("spatial") > 0, 1.0, 0.0).astype(f32)
    planes = [(e, halo[e].astype(f32) * inside) for e in range(3)]
    fill(vpad, x1, planes, 0, 2)
    x1[64:128, 768:] = x1_mid[:, 768:]
    hidden_of(x1, w1p, slope, picked)
    out_planes = x2.shape[0] // 16
    for o in range(out_planes):
        for tap in range(27):
            h, pair = 2 * o + tap // 9, tap % 9
            if h < 2:
                cells = picked[h * 144 + pair * 16 : h * 144 + (pair + 1) * 16, :]
            else:
                at = (h - 2) * 144 + pair * 16
                cells = picked_up[at : at + 16, :]
            x2[o * 16 : (o + 1) * 16, tap * LANES : (tap + 1) * LANES] = cells
    second_pre = jnp.concatenate(
        [dot(x2[...], w2[:, :LANES]), dot(x2[...], w2[:, LANES:])], 1
    )
    sig = sigmoid(second_pre)
    delta = cot[...] * slope_of(second_pre, sig)
    d2[...] = delta.astype(bf16)
    core = half_of(flat_index(spatial_count), bits)
    left, right = delta[:, :LANES], delta[:, LANES:]
    own_first[...] = jnp.concatenate(
        [jnp.where(core == 0, left, right), jnp.where(core == 0, right, left)], 1
    ).astype(bf16)
    second_taps(x2, own_first[...], keep, send, 0, SPLIT)
    clear(keep, send, SPLIT * LANES // 2)


def last_kernel(
    bits, spatial_count, x1_up, x1_low, slope_up, slope_low, x2, d2, own_first, w2,
    keep, send, g1,
):
    second_taps(x2, own_first[...], keep, send, SPLIT, 27)
    out_planes = x2.shape[0] // 16
    hidden_planes = 2 * out_planes + 1
    select = selection()
    spread = dot(d2[...], w2[...], ((1,), (1,)))
    coarse = spread.astype(bf16)
    fine = (spread - coarse.astype(f32)).astype(bf16)
    deltas = []
    for h in range(hidden_planes):
        total = None
        for a in range(h % 2, 3, 2):
            o = (h - a) // 2
            if 0 <= o < out_planes:
                rows = slice(o * 16, (o + 1) * 16)
                stack = []
                for tap in range(a * 9, a * 9 + 9):
                    columns = slice(tap * LANES, (tap + 1) * LANES)
                    stack.append(jnp.concatenate([coarse[rows, columns], fine[rows, columns]], 1))
                both = dot(select, jnp.concatenate(stack, 0), ((0,), (0,)))
                part = both[:, :LANES] + both[:, LANES:]
                total = part if total is None else total + part
        rounded = total.astype(bf16).astype(f32)
        if h < 2:
            slope = slope_low[h * 64 : (h + 1) * 64]
        else:
            slope = slope_up[(h - 2) * 64 : (h - 1) * 64]
        deltas.append((rounded * slope).astype(bf16))
    d1_low, d1_up = jnp.concatenate(deltas[:2], 0), jnp.concatenate(deltas[2:], 0)
    for a in range(3):
        columns = slice(a * 768, (a + 1) * 768)
        grad = dot(d1_up, x1_up[:, columns], ((0,), (0,)))
        grad = (grad + dot(d1_low, x1_low[:, columns], ((0,), (0,)))).T
        for b in range(3):
            at = (a * 3 + b) * 192
            g1[at : at + 192, :] = grad[b * 256 + 64 : (b + 1) * 256]
    core = half_of(flat_index(spatial_count), bits)
    start, quarter = (27 - SPLIT) * LANES // 2, FIRST // 2
    for v in range(2):
        rows = slice(v * (keep.shape[0] // 2) + start, v * (keep.shape[0] // 2) + start + quarter)
        mine = pl.ds(pl.multiple_of(core * FIRST + v * quarter, 8), quarter)
        other = pl.ds(pl.multiple_of((1 - core) * FIRST + v * quarter, 8), quarter)
        keep[rows, :] = g1[mine, :]
        send[rows, :] = g1[other, :].astype(bf16)
    clear(keep, send, start + quarter)


def side_of(flat, orders, core, step):
    first, second = bit_of(flat, orders[0][step]), bit_of(flat, orders[1][step])
    return jnp.where(core == 0, first, second)


def reduce_kernel(orders, bits, step, spatial_count, keep, recv, kept, gone):
    half = keep.shape[0] // 2
    flat = flat_index(spatial_count)
    bit = side_of(flat, orders, half_of(flat, bits), step)
    mine = pl.ds(pl.multiple_of(bit * half, 16), half)
    other = pl.ds(pl.multiple_of((1 - bit) * half, 16), half)
    kept[...] = keep[mine, :] + recv[mine, :].astype(f32)
    gone[...] = (keep[other, :] + recv[other, :].astype(f32)).astype(bf16)


def sum_kernel(keep, recv, out):
    out[...] = (keep[...].astype(f32) + recv[...].astype(f32)).astype(bf16)


def join_kernel(own, recv, out):
    half = own.shape[0]
    out[0:half, :] = own[...]
    out[half:, :] = recv[...]


def copy_kernel(got, out):
    out[...] = got[...]


def start_part(flat, side, orders, chunk, segments, last, part, wide, grad_first, grad_second, sems):
    steps = len(orders[0]) - 1
    bits = [side_of(flat, orders, side, s) for s in range(steps)]
    columns = pl.ds(pl.multiple_of(side * LANES, LANES), LANES)
    top = 1 - bits[0] if last else bits[0]
    copies = []
    for place in range(1 << (steps - 1)):
        position = jnp.int32(0)
        for s in range(1, steps):
            want = (place >> (steps - 1 - s)) & 1
            differs = (1 - bits[s]) if want else bits[s]
            position = position + differs * (1 << (steps - 1 - s))
        at = place * chunk
        rows = pl.ds(pl.multiple_of(position * chunk, 16), chunk)
        wide[at : at + chunk, :] = part[rows, :].astype(f32)
        for start, size, second, base in segments:
            low, high = max(start, at), min(start + size, at + chunk)
            if low >= high:
                continue
            to = top * size + base + low - start
            if second:
                target = grad_second.at[pl.ds(pl.multiple_of(to, 16), high - low), columns]
            else:
                to = pl.multiple_of(side * FIRST + to, 16)
                target = grad_first.at[pl.ds(to, high - low)]
            copy = pltpu.make_async_copy(wide.at[low:high], target, sems.at[len(copies)])
            copy.start()
            copies.append(copy)
    return copies


def final_kernel(bits, spatial_count, jobs, chained, *refs):
    count = len(jobs)
    tokens = refs[count + 2 * chained + 2 : -2 * count]
    grad_first, grad_second = refs[count + 2 * chained : count + 2 * chained + 2]
    wides, sems = refs[-2 * count : -count], refs[-count:]
    flat = flat_index(spatial_count)
    core = half_of(flat, bits)
    for token in tokens:
        token[...] = jnp.zeros(token.shape, f32)
    copies = []
    for index, (own, orders, chunk, segments, last) in enumerate(jobs):
        copies += start_part(
            flat, core if own else 1 - core, orders, chunk, segments, last,
            refs[index], wides[index], grad_first, grad_second, sems[index],
        )
    for copy in copies:
        copy.wait()


def body(spatial_count, sample_count, volume, w_first, w_second, cotangent):
    count = spatial_count * sample_count
    bits = count.bit_length() - 1
    core_bit = spatial_count.bit_length() - 1
    others = [bit for bit in range(bits) if bit != core_bit]
    turn, rest = others[:3], others[3:]
    orders = [
        [tuple(turn[i] for i in turns) + tuple(rest) for turns in lane] for lane in LANE_TURNS
    ]
    steps = len(others) - 1
    lanes = len(LANE_TURNS)
    unit = 16 << steps
    second_rest = (27 - SPLIT) * LANES // 2
    segments = [
        [(0, SPLIT * LANES // 2, True, 0)],
        [(0, second_rest, True, SPLIT * LANES), (second_rest, FIRST // 2, False, 0)],
    ]
    chunks = [-(-2 * sum(seg[1] for seg in lane) // unit) * 16 for lane in segments]

    def swap_core(array):
        return lax.ppermute(array, BOTH, [(i, i ^ (1 << core_bit)) for i in range(count)])

    def swap(array, lane, step):
        pairs = []
        for i in range(count):
            bit = orders[lane][i.bit_count() % 2][step]
            pairs.append((i, i ^ (1 << bit) ^ (1 << core_bit)))
        return lax.ppermute(array, BOTH, pairs)

    slab = volume[0]
    depth = slab.shape[0]
    out_planes = depth // 4
    up = 2 * out_planes - 1
    slab_cot = cotangent[0]
    outside = pl.BlockSpec(memory_space=pl.ANY)
    far = pltpu.HBM
    face = slab[-3:]
    halo = lax.ppermute(
        face, "spatial", [(i, (i + 1) % spatial_count) for i in range(spatial_count)]
    )
    w2 = w_second
    x1_mid, x1_up, w1p = call(
        load_kernel,
        [
            ((64, 9 * 256), bf16),
            ((up * 64, 9 * 256), bf16),
            ((9 * 256, 128), bf16),
        ],
        pltpu.with_memory_space_constraint(slab, far),
        pltpu.with_memory_space_constraint(w_first, far),
        specs=[outside] * 2,
        scratch=[
            pltpu.VMEM(slab.shape, bf16),
            pltpu.VMEM(w_first.shape, bf16),
            pltpu.VMEM((depth - 1, 8, 32, LANES), f32),
            pltpu.SemaphoreType.DMA((3,)),
        ],
        after=(face,),
        cost=STEP_COST,
    )
    cells = out_planes * 16
    slope_up, picked_up, cot = call(
        upper_kernel,
        [
            ((up * 64, LANES), f32),
            ((up * 144, LANES), bf16),
            ((cells, 256), f32),
        ],
        x1_up,
        w1p,
        pltpu.with_memory_space_constraint(slab_cot, far),
        specs=[full(None), full(None), outside],
        scratch=[pltpu.VMEM(slab_cot.shape, bf16), pltpu.SemaphoreType.DMA((2,))],
        cost=pl.CostEstimate(flops=4 * 10**8, bytes_accessed=10**7, transcendentals=0),
    )
    rows = [chunk << steps for chunk in chunks]
    keep0, send0, x1_low, slope_low, x2, d2, own_first = call(
        functools.partial(lower_kernel, bits, spatial_count),
        [
            ((rows[0], LANES), f32),
            ((rows[0], LANES), bf16),
            ((128, 9 * 256), bf16),
            ((128, LANES), f32),
            ((cells, 27 * LANES), bf16),
            ((cells, 256), bf16),
            ((cells, 256), bf16),
        ],
        halo,
        x1_mid,
        w1p,
        picked_up,
        w2,
        cot,
        scratch=[pltpu.VMEM((3, 8, 32, LANES), f32), pltpu.VMEM((288, LANES), bf16)],
    )
    recv0 = swap_core(send0)
    keep1, send1 = call(
        functools.partial(last_kernel, bits, spatial_count),
        [((rows[1], LANES), f32), ((rows[1], LANES), bf16)],
        x1_up,
        x1_low,
        slope_up,
        slope_low,
        x2,
        d2,
        own_first,
        w2,
        scratch=[pltpu.VMEM((2 * FIRST, LANES), f32)],
        cost=pl.CostEstimate(flops=10**9, bytes_accessed=10**7, transcendentals=0),
    )
    recv1 = swap_core(send1)
    keep, recv = [keep0, keep1], [recv0, recv1]
    last = send1
    for step in range(steps):
        for lane in range(lanes):
            half = keep[lane].shape[0] // 2
            keep[lane], last = call(
                functools.partial(reduce_kernel, orders[lane], bits, step, spatial_count),
                [((half, LANES), f32), ((half, LANES), bf16)],
                keep[lane],
                recv[lane],
                after=(last,),
                cost=STEP_COST,
            )
            recv[lane] = swap(last, lane, step)
    for turn in range(2):
        for lane in range(lanes):
            shape = [((chunks[lane], LANES), bf16)]
            last = call(sum_kernel, shape, keep[lane], recv[lane], after=(last,), cost=STEP_COST)[0]
            keep[lane], recv[lane] = last, swap(last, lane, steps - turn)
    for step in reversed(range(1, steps)):
        for lane in range(lanes):
            shape = [((2 * keep[lane].shape[0], LANES), bf16)]
            last = call(
                join_kernel, shape, keep[lane], recv[lane], after=(last,), cost=STEP_COST
            )[0]
            keep[lane], recv[lane] = last, swap(last, lane, step - 1)
    held = [[keep[lane], None, None, None] for lane in range(lanes)]
    shapes = [jax.ShapeDtypeStruct((2 * FIRST, LANES), f32)]
    shapes += [jax.ShapeDtypeStruct((SECOND, 2 * LANES), f32)]
    token_shape = [jax.ShapeDtypeStruct((8, LANES), f32)]
    grads = []

    def write(group, grads, token):
        parts = [held[lane][which] for lane, which in group]
        jobs = [
            (which < 2, orders[lane], chunks[lane], segments[lane], which % 2 == 1)
            for lane, which in group
        ]
        return pl.pallas_call(
            functools.partial(final_kernel, bits, spatial_count, jobs, bool(grads)),
            out_shape=shapes + token_shape * token,
            in_specs=[full(part.shape) for part in parts] + [outside] * len(grads),
            out_specs=[outside] * 2 + [full(None)] * token,
            scratch_shapes=[pltpu.VMEM((rows[lane] // 2, LANES), f32) for lane, _ in group]
            + [pltpu.SemaphoreType.DMA(((1 << steps) + 1,)) for _ in group],
            input_output_aliases={len(parts): 0, len(parts) + 1: 1} if grads else {},
            compiler_params=params(),
            cost_estimate=STEP_COST,
        )(*parts, *grads)

    def copied(array, after):
        return call(copy_kernel, [(array.shape, bf16)], array, after=after, cost=STEP_COST)[0]

    for lane, group in enumerate(WRITES[:lanes]):
        *grads, token = write(group, grads, 1)
        if lane == 0:
            for part in held:
                part[2] = swap_core(copied(part[0], (token,)))
        last = copied(recv[lane], (last, token))
        held[lane][1], held[lane][3] = last, swap_core(last)
    for group in WRITES[lanes:]:
        grads = write(group, grads, 0)
    return grads


def solution(mesh):
    sizes = dict(mesh.shape)

    def run(*args):
        return tuple(body(sizes["spatial"], sizes["sample"], *args))

    return jax.shard_map(
        run,
        mesh=mesh,
        in_specs=(P("sample", "spatial", None, None), P(), P(), P("sample", "spatial", None, None)),
        out_specs=(P(), P()),
        check_vma=False,
    )
```

```python
import functools

import jax
import jax.numpy as jnp
from jax import lax
from jax.experimental import pallas as pl
from jax.experimental.pallas import tpu as pltpu
from jax.sharding import PartitionSpec as P

BOTH = ("sample", "spatial")
LANES = 128
SECOND, FIRST = 3456, 864
VMEM_BYTES = 32 * 1024 * 1024
SPLIT = 17
LANE_TURNS = (((0, 1, 2), (1, 2, 0)), ((2, 0, 1), (1, 2, 0)))
f32, bf16 = jnp.float32, jnp.bfloat16

WRITES = (((0, 0), (1, 0)), ((0, 2), (1, 2), (0, 1)), ((0, 3), (1, 1)), ((1, 3),))
STEP_COST = pl.CostEstimate(flops=4 * 10**9, bytes_accessed=8 * 10**7, transcendentals=0)


def full(shape):
    return pl.BlockSpec(memory_space=pltpu.VMEM)


def params():
    return pltpu.CompilerParams(vmem_limit_bytes=VMEM_BYTES)


def call(kernel, outs, *args, specs=None, scratch=(), cost=None, after=()):
    shapes = [jax.ShapeDtypeStruct(s, d) for s, d in outs]
    count = len(args)

    def run(*refs):
        kernel(*refs[:count], *refs[count + len(after) :])

    return pl.pallas_call(
        run,
        out_shape=shapes,
        in_specs=(specs or [full(a.shape) for a in args])
        + [pl.BlockSpec(memory_space=pl.ANY)] * len(after),
        out_specs=[full(s.shape) for s in shapes],
        scratch_shapes=scratch,
        compiler_params=params(),
        cost_estimate=cost,
    )(*args, *after)


def flat_index(spatial_count):
    return lax.axis_index("sample") * spatial_count + lax.axis_index("spatial")


def bit_of(value, bit):
    return lax.rem(lax.div(value, jnp.int32(1 << bit)), jnp.int32(2))


def half_of(flat, bits):
    total = jnp.int32(0)
    for bit in range(bits):
        total = total + bit_of(flat, bit)
    return lax.rem(total, jnp.int32(2))


def sigmoid(value):
    return 1.0 / (1.0 + jnp.exp(-value))


def slope_of(value, sig):
    return sig * (1.0 + value * (1.0 - sig))


def dot(a, b, dims=((1,), (0,))):
    return lax.dot_general(a, b, (dims, ((), ())), preferred_element_type=f32)


def selection():
    row = lax.broadcasted_iota(jnp.int32, (144, 64), 0)
    col = lax.broadcasted_iota(jnp.int32, (144, 64), 1)
    pair, cell = lax.div(row, 16), lax.rem(row, 16)
    b, c = lax.div(pair, 3), lax.rem(pair, 3)
    k, j = lax.div(cell, 4), lax.rem(cell, 4)
    x, y = lax.div(col, 8), lax.rem(col, 8)
    hit = (x == 2 * k + c - 1) & (y == 2 * j + b - 1)
    return hit.astype(f32).astype(bf16)


def fill(vpad, x1, planes, first_hidden, count):
    for index, (e, plane) in enumerate(planes):
        vpad[index, :, 0:8, :] = jnp.zeros((8, 8, LANES), f32)
        for kt in range(8):
            vpad[index, kt, 8:24, :] = plane[:, kt * LANES : (kt + 1) * LANES].astype(f32)
    for index, (e, plane) in enumerate(planes):
        for b in range(3):
            tiles = [jnp.zeros((8, LANES), f32)]
            for kt in range(8):
                tiles.append(vpad[index, kt, pl.ds(7 + b, 8, stride=2), :])
            for kk in range(4):
                left = jnp.concatenate([tiles[2 * kk], tiles[2 * kk + 1]], 0).astype(bf16)
                right = jnp.concatenate([tiles[2 * kk + 1], tiles[2 * kk + 2]], 0).astype(bf16)
                for a in range(e % 2, 3, 2):
                    h = (e - a) // 2 - first_hidden
                    if 0 <= h < count:
                        rows = slice(h * 64 + kk * 16, h * 64 + kk * 16 + 16)
                        col = (a * 3 + b) * 256
                        x1[rows, col : col + LANES] = left
                        x1[rows, col + LANES : col + 2 * LANES] = right


def load_kernel(vol_hbm, w1_hbm, x1_mid, x1, w1p, vol, w1, vpad, sems):
    loads = [
        pltpu.make_async_copy(vol_hbm, vol, sems.at[0]),
        pltpu.make_async_copy(w1_hbm, w1, sems.at[1]),
    ]
    for load in loads:
        load.start()
    loads[0].wait()
    depth = vol.shape[0]
    fill(vpad, x1_mid, [(e, vol[e - 3]) for e in (3, 4)], 1, 1)
    planes = [(e, vol[e - 3]) for e in range(4, depth + 3)]
    fill(vpad, x1, planes, 2, x1.shape[0] // 64)
    loads[1].wait()
    for ab in range(9):
        w1p[ab * 256 : ab * 256 + 64, :] = jnp.zeros((64, 128), bf16)
        w1p[ab * 256 + 64 : (ab + 1) * 256, :] = w1[ab * 192 : (ab + 1) * 192, :]


def hidden_of(x1, w1p, slope, picked):
    rows = x1.shape[0]
    middle = rows // 128 * 64
    cuts = [(0, middle), (middle, rows)] if middle else [(0, rows)]
    first_pre = jnp.concatenate([dot(x1[low:high, :], w1p[...]) for low, high in cuts], 0)
    sig = sigmoid(first_pre)
    hidden = (first_pre * sig).astype(bf16)
    slope[...] = slope_of(first_pre, sig)
    select = selection()
    planes = hidden.shape[0] // 64
    for h in range(0, planes, 2):
        pair = [hidden[g * 64 : (g + 1) * 64] for g in range(h, min(h + 2, planes))]
        cells = dot(select, jnp.concatenate(pair, 1)).astype(bf16)
        for g in range(len(pair)):
            at = (h + g) * 144
            picked[at : at + 144, :] = cells[:, g * LANES : (g + 1) * LANES]


def upper_kernel(x1, w1p, cot_hbm, slope, picked, cot, cot_in, sems):
    loads = [
        pltpu.make_async_copy(cot_hbm, cot_in, sems.at[0]),
    ]
    for load in loads:
        load.start()
    hidden_of(x1, w1p, slope, picked)
    loads[0].wait()
    row = lax.broadcasted_iota(jnp.int32, (16, 4), 0)
    col = lax.broadcasted_iota(jnp.int32, (16, 4), 1)
    for o in range(cot_in.shape[0]):
        cells = None
        for k in range(4):
            place = (row == 4 * k + col).astype(f32).astype(bf16)
            part = dot(place, cot_in[o, :, k * 256 : (k + 1) * 256])
            cells = part if cells is None else cells + part
        cot[o * 16 : (o + 1) * 16, :] = cells


def second_taps(x2, own_first, keep, send, first_tap, last_tap):
    columns = slice(first_tap * LANES, last_tap * LANES)
    rows = (last_tap - first_tap) * LANES // 2
    half = keep.shape[0] // 2
    grad = dot(x2[:, columns], own_first, ((0,), (0,)))
    for v in range(2):
        keep[v * half : v * half + rows, :] = grad[v * rows : (v + 1) * rows, :LANES]
        send[v * half : v * half + rows, :] = grad[v * rows : (v + 1) * rows, LANES:].astype(bf16)


def clear(keep, send, start):
    half = keep.shape[0] // 2
    if start < half:
        for v in range(2):
            rows = slice(v * half + start, (v + 1) * half)
            keep[rows, :] = jnp.zeros((half - start, LANES), f32)
            send[rows, :] = jnp.zeros((half - start, LANES), bf16)


def lower_kernel(
    bits, spatial_count, halo, x1_mid, w1p, picked_up, w2, cot,
    keep, send, x1, slope, x2, d2, own_first, vpad, picked,
):
    inside = jnp.where(lax.axis_index("spatial") > 0, 1.0, 0.0).astype(f32)
    planes = [(e, halo[e].astype(f32) * inside) for e in range(3)]
    fill(vpad, x1, planes, 0, 2)
    x1[64:128, 768:] = x1_mid[:, 768:]
    hidden_of(x1, w1p, slope, picked)
    out_planes = x2.shape[0] // 16
    for o in range(out_planes):
        for tap in range(27):
            h, pair = 2 * o + tap // 9, tap % 9
            if h < 2:
                cells = picked[h * 144 + pair * 16 : h * 144 + (pair + 1) * 16, :]
            else:
                at = (h - 2) * 144 + pair * 16
                cells = picked_up[at : at + 16, :]
            x2[o * 16 : (o + 1) * 16, tap * LANES : (tap + 1) * LANES] = cells
    second_pre = jnp.concatenate(
        [dot(x2[...], w2[:, :LANES]), dot(x2[...], w2[:, LANES:])], 1
    )
    sig = sigmoid(second_pre)
    delta = cot[...] * slope_of(second_pre, sig)
    d2[...] = delta.astype(bf16)
    core = half_of(flat_index(spatial_count), bits)
    left, right = delta[:, :LANES], delta[:, LANES:]
    own_first[...] = jnp.concatenate(
        [jnp.where(core == 0, left, right), jnp.where(core == 0, right, left)], 1
    ).astype(bf16)
    second_taps(x2, own_first[...], keep, send, 0, SPLIT)
    clear(keep, send, SPLIT * LANES // 2)


def last_kernel(
    bits, spatial_count, x1_up, x1_low, slope_up, slope_low, x2, d2, own_first, w2,
    keep, send, g1,
):
    second_taps(x2, own_first[...], keep, send, SPLIT, 27)
    out_planes = x2.shape[0] // 16
    hidden_planes = 2 * out_planes + 1
    select = selection()
    spread = dot(d2[...], w2[...], ((1,), (1,)))
    coarse = spread.astype(bf16)
    fine = (spread - coarse.astype(f32)).astype(bf16)
    deltas = []
    for h in range(hidden_planes):
        total = None
        for a in range(h % 2, 3, 2):
            o = (h - a) // 2
            if 0 <= o < out_planes:
                rows = slice(o * 16, (o + 1) * 16)
                stack = []
                for tap in range(a * 9, a * 9 + 9):
                    columns = slice(tap * LANES, (tap + 1) * LANES)
                    stack.append(jnp.concatenate([coarse[rows, columns], fine[rows, columns]], 1))
                both = dot(select, jnp.concatenate(stack, 0), ((0,), (0,)))
                part = both[:, :LANES] + both[:, LANES:]
                total = part if total is None else total + part
        rounded = total.astype(bf16).astype(f32)
        if h < 2:
            slope = slope_low[h * 64 : (h + 1) * 64]
        else:
            slope = slope_up[(h - 2) * 64 : (h - 1) * 64]
        deltas.append((rounded * slope).astype(bf16))
    d1_low, d1_up = jnp.concatenate(deltas[:2], 0), jnp.concatenate(deltas[2:], 0)
    for a in range(3):
        for b in range(3):
            at, block = (a * 3 + b) * 192, slice(a * 768 + b * 256, a * 768 + (b + 1) * 256)
            grad = dot(d1_up, x1_up[:, block], ((0,), (0,)))
            grad = (grad + dot(d1_low, x1_low[:, block], ((0,), (0,)))).T
            g1[at : at + 192, :] = grad[64:256]
    core = half_of(flat_index(spatial_count), bits)
    start, quarter = (27 - SPLIT) * LANES // 2, FIRST // 2
    for v in range(2):
        rows = slice(v * (keep.shape[0] // 2) + start, v * (keep.shape[0] // 2) + start + quarter)
        mine = pl.ds(pl.multiple_of(core * FIRST + v * quarter, 8), quarter)
        other = pl.ds(pl.multiple_of((1 - core) * FIRST + v * quarter, 8), quarter)
        keep[rows, :] = g1[mine, :]
        send[rows, :] = g1[other, :].astype(bf16)
    clear(keep, send, start + quarter)


def side_of(flat, orders, core, step):
    first, second = bit_of(flat, orders[0][step]), bit_of(flat, orders[1][step])
    return jnp.where(core == 0, first, second)


def reduce_kernel(orders, bits, step, spatial_count, keep, recv, kept, gone):
    half = keep.shape[0] // 2
    flat = flat_index(spatial_count)
    bit = side_of(flat, orders, half_of(flat, bits), step)
    mine = pl.ds(pl.multiple_of(bit * half, 16), half)
    other = pl.ds(pl.multiple_of((1 - bit) * half, 16), half)
    kept[...] = keep[mine, :] + recv[mine, :].astype(f32)
    gone[...] = (keep[other, :] + recv[other, :].astype(f32)).astype(bf16)


def sum_kernel(keep, recv, out):
    out[...] = (keep[...].astype(f32) + recv[...].astype(f32)).astype(bf16)


def join_kernel(own, recv, out):
    half = own.shape[0]
    out[0:half, :] = own[...]
    out[half:, :] = recv[...]


def copy_kernel(got, out):
    out[...] = got[...]


def start_part(flat, side, orders, chunk, segments, last, part, wide, grad_first, grad_second, sems):
    steps = len(orders[0]) - 1
    bits = [side_of(flat, orders, side, s) for s in range(steps)]
    columns = pl.ds(pl.multiple_of(side * LANES, LANES), LANES)
    top = 1 - bits[0] if last else bits[0]
    copies = []
    for place in range(1 << (steps - 1)):
        position = jnp.int32(0)
        for s in range(1, steps):
            want = (place >> (steps - 1 - s)) & 1
            differs = (1 - bits[s]) if want else bits[s]
            position = position + differs * (1 << (steps - 1 - s))
        at = place * chunk
        rows = pl.ds(pl.multiple_of(position * chunk, 16), chunk)
        wide[at : at + chunk, :] = part[rows, :].astype(f32)
        for start, size, second, base in segments:
            low, high = max(start, at), min(start + size, at + chunk)
            if low >= high:
                continue
            to = top * size + base + low - start
            if second:
                target = grad_second.at[pl.ds(pl.multiple_of(to, 16), high - low), columns]
            else:
                to = pl.multiple_of(side * FIRST + to, 16)
                target = grad_first.at[pl.ds(to, high - low)]
            copy = pltpu.make_async_copy(wide.at[low:high], target, sems.at[len(copies)])
            copy.start()
            copies.append(copy)
    return copies


def final_kernel(bits, spatial_count, jobs, chained, *refs):
    count = len(jobs)
    tokens = refs[count + 2 * chained + 2 : -2 * count]
    grad_first, grad_second = refs[count + 2 * chained : count + 2 * chained + 2]
    wides, sems = refs[-2 * count : -count], refs[-count:]
    flat = flat_index(spatial_count)
    core = half_of(flat, bits)
    for token in tokens:
        token[...] = jnp.zeros(token.shape, f32)
    copies = []
    for index, (own, orders, chunk, segments, last) in enumerate(jobs):
        copies += start_part(
            flat, core if own else 1 - core, orders, chunk, segments, last,
            refs[index], wides[index], grad_first, grad_second, sems[index],
        )
    for copy in copies:
        copy.wait()


def body(spatial_count, sample_count, volume, w_first, w_second, cotangent):
    count = spatial_count * sample_count
    bits = count.bit_length() - 1
    core_bit = spatial_count.bit_length() - 1
    others = [bit for bit in range(bits) if bit != core_bit]
    turn, rest = others[:3], others[3:]
    orders = [
        [tuple(turn[i] for i in turns) + tuple(rest) for turns in lane] for lane in LANE_TURNS
    ]
    steps = len(others) - 1
    lanes = len(LANE_TURNS)
    unit = 16 << steps
    second_rest = (27 - SPLIT) * LANES // 2
    segments = [
        [(0, SPLIT * LANES // 2, True, 0)],
        [(0, second_rest, True, SPLIT * LANES), (second_rest, FIRST // 2, False, 0)],
    ]
    chunks = [-(-2 * sum(seg[1] for seg in lane) // unit) * 16 for lane in segments]

    def swap_core(array):
        return lax.ppermute(array, BOTH, [(i, i ^ (1 << core_bit)) for i in range(count)])

    def swap(array, lane, step):
        pairs = []
        for i in range(count):
            bit = orders[lane][i.bit_count() % 2][step]
            pairs.append((i, i ^ (1 << bit) ^ (1 << core_bit)))
        return lax.ppermute(array, BOTH, pairs)

    slab = volume[0]
    depth = slab.shape[0]
    out_planes = depth // 4
    up = 2 * out_planes - 1
    slab_cot = cotangent[0]
    outside = pl.BlockSpec(memory_space=pl.ANY)
    far = pltpu.HBM
    face = slab[-3:]
    halo = lax.ppermute(
        face, "spatial", [(i, (i + 1) % spatial_count) for i in range(spatial_count)]
    )
    w2 = w_second
    x1_mid, x1_up, w1p = call(
        load_kernel,
        [
            ((64, 9 * 256), bf16),
            ((up * 64, 9 * 256), bf16),
            ((9 * 256, 128), bf16),
        ],
        pltpu.with_memory_space_constraint(slab, far),
        pltpu.with_memory_space_constraint(w_first, far),
        specs=[outside] * 2,
        scratch=[
            pltpu.VMEM(slab.shape, bf16),
            pltpu.VMEM(w_first.shape, bf16),
            pltpu.VMEM((depth - 1, 8, 32, LANES), f32),
            pltpu.SemaphoreType.DMA((3,)),
        ],
        after=(face,),
        cost=STEP_COST,
    )
    cells = out_planes * 16
    slope_up, picked_up, cot = call(
        upper_kernel,
        [
            ((up * 64, LANES), f32),
            ((up * 144, LANES), bf16),
            ((cells, 256), f32),
        ],
        x1_up,
        w1p,
        pltpu.with_memory_space_constraint(slab_cot, far),
        specs=[full(None), full(None), outside],
        scratch=[pltpu.VMEM(slab_cot.shape, bf16), pltpu.SemaphoreType.DMA((2,))],
        cost=pl.CostEstimate(flops=4 * 10**8, bytes_accessed=10**7, transcendentals=0),
    )
    rows = [chunk << steps for chunk in chunks]
    keep0, send0, x1_low, slope_low, x2, d2, own_first = call(
        functools.partial(lower_kernel, bits, spatial_count),
        [
            ((rows[0], LANES), f32),
            ((rows[0], LANES), bf16),
            ((128, 9 * 256), bf16),
            ((128, LANES), f32),
            ((cells, 27 * LANES), bf16),
            ((cells, 256), bf16),
            ((cells, 256), bf16),
        ],
        halo,
        x1_mid,
        w1p,
        picked_up,
        w2,
        cot,
        scratch=[pltpu.VMEM((3, 8, 32, LANES), f32), pltpu.VMEM((288, LANES), bf16)],
    )
    recv0 = swap_core(send0)
    keep1, send1 = call(
        functools.partial(last_kernel, bits, spatial_count),
        [((rows[1], LANES), f32), ((rows[1], LANES), bf16)],
        x1_up,
        x1_low,
        slope_up,
        slope_low,
        x2,
        d2,
        own_first,
        w2,
        scratch=[pltpu.VMEM((2 * FIRST, LANES), f32)],
        cost=pl.CostEstimate(flops=10**9, bytes_accessed=10**7, transcendentals=0),
    )
    recv1 = swap_core(send1)
    keep, recv = [keep0, keep1], [recv0, recv1]
    last = send1
    for step in range(steps):
        for lane in range(lanes):
            half = keep[lane].shape[0] // 2
            keep[lane], last = call(
                functools.partial(reduce_kernel, orders[lane], bits, step, spatial_count),
                [((half, LANES), f32), ((half, LANES), bf16)],
                keep[lane],
                recv[lane],
                after=(last,),
                cost=STEP_COST,
            )
            recv[lane] = swap(last, lane, step)
    for turn in range(2):
        for lane in range(lanes):
            shape = [((chunks[lane], LANES), bf16)]
            last = call(sum_kernel, shape, keep[lane], recv[lane], after=(last,), cost=STEP_COST)[0]
            keep[lane], recv[lane] = last, swap(last, lane, steps - turn)
    for step in reversed(range(1, steps)):
        for lane in range(lanes):
            shape = [((2 * keep[lane].shape[0], LANES), bf16)]
            last = call(
                join_kernel, shape, keep[lane], recv[lane], after=(last,), cost=STEP_COST
            )[0]
            keep[lane], recv[lane] = last, swap(last, lane, step - 1)
    held = [[keep[lane], None, None, None] for lane in range(lanes)]
    shapes = [jax.ShapeDtypeStruct((2 * FIRST, LANES), f32)]
    shapes += [jax.ShapeDtypeStruct((SECOND, 2 * LANES), f32)]
    token_shape = [jax.ShapeDtypeStruct((8, LANES), f32)]
    grads = []

    def write(group, grads, token):
        parts = [held[lane][which] for lane, which in group]
        jobs = [
            (which < 2, orders[lane], chunks[lane], segments[lane], which % 2 == 1)
            for lane, which in group
        ]
        return pl.pallas_call(
            functools.partial(final_kernel, bits, spatial_count, jobs, bool(grads)),
            out_shape=shapes + token_shape * token,
            in_specs=[full(part.shape) for part in parts] + [outside] * len(grads),
            out_specs=[outside] * 2 + [full(None)] * token,
            scratch_shapes=[pltpu.VMEM((rows[lane] // 2, LANES), f32) for lane, _ in group]
            + [pltpu.SemaphoreType.DMA(((1 << steps) + 1,)) for _ in group],
            input_output_aliases={len(parts): 0, len(parts) + 1: 1} if grads else {},
            compiler_params=params(),
            cost_estimate=STEP_COST,
        )(*parts, *grads)

    def copied(array, after):
        return call(copy_kernel, [(array.shape, bf16)], array, after=after, cost=STEP_COST)[0]

    for lane, group in enumerate(WRITES[:lanes]):
        *grads, token = write(group, grads, 1)
        if lane == 0:
            for part in held:
                part[2] = swap_core(copied(part[0], (token,)))
        last = copied(recv[lane], (last, token))
        held[lane][1], held[lane][3] = last, swap_core(last)
    for group in WRITES[lanes:]:
        grads = write(group, grads, 0)
    return grads


def solution(mesh):
    sizes = dict(mesh.shape)

    def run(*args):
        return tuple(body(sizes["spatial"], sizes["sample"], *args))

    return jax.shard_map(
        run,
        mesh=mesh,
        in_specs=(P("sample", "spatial", None, None), P(), P(), P("sample", "spatial", None, None)),
        out_specs=(P(), P()),
        check_vma=False,
    )
```
